512 devices in a mesh: row: 32 (over z_lo, y), col: 16 (over x, z_hi, core).
Axes of the slice: x: 4, y: 8, z: 8 (z_hi: 2, z_lo: 4; z = z_hi * 4 + z_lo), core: 2. Of those that a mesh axis runs over, the one named last changes fastest.
Arguments:
- a_vals: bfloat16 [32, 16, 4, 5, 9216], P('row', 'col'), may hold values from -1.5 to 1.5
- a_cols: int32 [32, 16, 4, 5], P('row', 'col'), may hold values from 0 to 7, as said below
- a_count: int32 [32, 16, 4], P('row', 'col'), may hold values from 1 to 5, as said below
- b_vals: bfloat16 [32, 16, 8, 2, 9216], P('row', 'col'), may hold values from -1.5 to 1.5, as said below
- b_cols: int32 [32, 16, 8, 2], P('row', 'col'), may hold values from 0 to 7, as said below
- b_count: int32 [32, 16, 8], P('row', 'col'), may hold values from 0 to 2, as said below
Outputs:
- next_sign: bfloat16 [12288, 12288], P('row', 'col')
The draws below stay inside these ranges and needn't reach their ends.
Inputs may be any that keep to these rules, and one draw needn't show every extreme that they name: `a_cols`: the block columns within one block row of a tile are distinct. `a_count`: in every grid row one tile holds 5 blocks in each of its block rows. `b_vals`: entry [u, c] equals entry [u mod Q, c], Q the number of grid columns. `b_cols`: the block columns within one block row of a tile are distinct; entry [u, c] equals entry [u mod Q, c], Q the number of grid columns. `b_count`: in every grid column one tile holds 2 blocks in each of its block rows; entry [u, c] equals entry [u mod Q, c], Q the number of grid columns.
All inputs are finite; a program needn't handle non-finite values.
Results may differ from the reference program's by a relative error of at most 0.001.
Values may be sent and summed in bfloat16 or wider, within the bound.
A program may use at most 64 MiB of HBM per device.

```python
import jax
import jax.numpy as jnp
from jax import lax

BLOCK = 96
RB = 4
A_SLOTS = 5
B_SLOTS = 2
CB = 8
N_ROW = 32
N_COL = 16


def repeat_rows(values):
    return jnp.tile(values, (N_ROW // N_COL,) + (1,) * (values.ndim - 1))


def draw_a_cols(key, part):
    key = jax.random.fold_in(key, 11)
    subkeys = jax.random.split(key, N_ROW * N_COL * RB)
    chosen = jax.vmap(lambda subkey: jax.random.permutation(subkey, CB)[:A_SLOTS])(subkeys)
    return chosen.reshape(N_ROW, N_COL, RB, A_SLOTS).astype(jnp.int32)


def draw_a_count(key, part):
    key = jax.random.fold_in(key, 12)
    first, second = jax.random.split(key)
    base = jax.random.randint(first, (N_ROW, N_COL, RB), 1, max(2, A_SLOTS // 2) + 1)
    dense_col = jax.random.randint(second, (N_ROW, 1, 1), 0, N_COL)
    full = jnp.arange(N_COL, dtype=jnp.int32)[None, :, None] == dense_col
    return jnp.where(full, A_SLOTS, base).astype(jnp.int32)


def draw_b_vals(key, part):
    key = jax.random.fold_in(key, 13)
    first = jax.random.fold_in(key, 0)
    shape = (N_COL, N_COL, CB, B_SLOTS, BLOCK * BLOCK)
    values = 0.3 * jax.random.normal(first, shape, jnp.float32)
    values = jnp.clip(values, -1.5, 1.5)
    return repeat_rows(values).astype(jnp.bfloat16)


def draw_b_cols(key, part):
    key = jax.random.fold_in(key, 14)
    subkeys = jax.random.split(key, N_COL * N_COL * CB)
    chosen = jax.vmap(lambda subkey: jax.random.permutation(subkey, CB)[:B_SLOTS])(subkeys)
    return repeat_rows(chosen.reshape(N_COL, N_COL, CB, B_SLOTS).astype(jnp.int32))


def draw_b_count(key, part):
    key = jax.random.fold_in(key, 15)
    first, second = jax.random.split(key)
    base = jax.random.randint(first, (N_COL, N_COL, CB), 0, B_SLOTS + 1)
    dense_row = jax.random.randint(second, (1, N_COL, 1), 0, N_COL)
    full = jnp.arange(N_COL, dtype=jnp.int32)[:, None, None] == dense_row
    return repeat_rows(jnp.where(full, B_SLOTS, base).astype(jnp.int32))


def block_scale(rng, extent, shards, least, top_value):
    loudness, own = 1.0, jax.random.fold_in(rng, 6)
    for dim, blocks in shards:
        heights = jnp.exp(jax.random.uniform(jax.random.fold_in(own, dim), (blocks,), jnp.float32, least / len(shards), top_value / len(shards)))
        loudness = loudness * jnp.repeat(heights, extent[dim] // blocks).reshape([-1 if axis == dim else 1 for axis in range(len(extent))])
    return loudness


def gaussian(own_key, extent, scale, reach, shards=(), kind=jnp.bfloat16):
    gain = block_scale(own_key, extent, shards, -0.22, 0.18) if shards else 1.0
    values = jax.random.normal(own_key, extent, jnp.float32) * scale * gain
    return jnp.minimum(jnp.maximum(values, -reach), reach).astype(kind)


def setup_inputs(seed: int = 0) -> dict:
    keys = jax.random.split(jax.random.key(seed), 7)
    return {
        "a_vals": gaussian(keys[0], (N_ROW, N_COL, RB, A_SLOTS, BLOCK * BLOCK), 0.3, 1.5, ((0, 32), (1, 16))),
        "a_cols": draw_a_cols(jax.random.fold_in(keys[6], 71), 0),
        "a_count": draw_a_count(jax.random.fold_in(keys[6], 71), 0),
        "b_vals": draw_b_vals(jax.random.fold_in(keys[6], 71), 0),
        "b_cols": draw_b_cols(jax.random.fold_in(keys[6], 71), 0),
        "b_count": draw_b_count(jax.random.fold_in(keys[6], 71), 0),
    }


def tile_term(a_blocks, a_where, a_number, b_blocks, b_where, b_number):
    block_rows, a_slots = a_where.shape
    block_cols, b_slots = b_where.shape
    a_live = jnp.arange(a_slots, dtype=jnp.int32)[None, :] < a_number[:, None]
    b_live = jnp.arange(b_slots, dtype=jnp.int32)[None, :] < b_number[:, None]
    partner_cols = b_where[a_where]
    partner_live = b_live[a_where] & a_live[:, :, None]
    targets = jnp.arange(block_cols, dtype=jnp.int32)
    matches = (partner_cols[..., None] == targets) & partner_live[..., None]
    flat_slot = a_where[..., None] * b_slots + jnp.arange(b_slots, dtype=jnp.int32)
    picked = jnp.sum(jnp.where(matches, flat_slot[..., None], 0), axis=2)
    slot_index = jnp.where(jnp.any(matches, axis=2), picked, block_cols * b_slots).astype(jnp.int32)
    flat_width = b_blocks.shape[-1]
    padded = jnp.concatenate([b_blocks.reshape(block_cols * b_slots, flat_width), jnp.zeros((1, flat_width), b_blocks.dtype)], axis=0)
    b_panel = padded[slot_index].reshape(block_rows, a_slots, block_cols, BLOCK, BLOCK)
    blocks = a_blocks.reshape(block_rows, a_slots, BLOCK, BLOCK)
    return jnp.einsum("ipxk,ipjky->ixjy", blocks.astype(jnp.float32), b_panel.astype(jnp.float32), precision=lax.Precision.HIGHEST)


def own_dense(a_blocks, a_where, a_number, block_cols):
    block_rows, a_slots = a_where.shape
    a_live = jnp.arange(a_slots, dtype=jnp.int32)[None, :] < a_number[:, None]
    placing = ((a_where[..., None] == jnp.arange(block_cols, dtype=jnp.int32)) & a_live[..., None]).astype(jnp.float32)
    blocks = a_blocks.reshape(block_rows, a_slots, BLOCK, BLOCK).astype(jnp.float32)
    return jnp.einsum("ipj,ipxy->ixjy", placing, blocks, precision=lax.Precision.HIGHEST)


def reference(a_vals, a_cols, a_count, b_vals, b_cols, b_count):
    grid_rows = a_cols.shape[0]
    grid_cols = a_cols.shape[1]
    block_rows = a_cols.shape[2]
    block_cols = b_cols.shape[2]

    def one_tile(flat_index):
        row_at = flat_index // grid_cols
        col_at = flat_index % grid_cols

        def add_term(summed, inner):
            a_entry = (inner - row_at) % grid_cols
            b_entry = (inner - col_at) % grid_cols
            term = tile_term(a_vals[row_at, a_entry], a_cols[row_at, a_entry], a_count[row_at, a_entry],
                             b_vals[b_entry, col_at], b_cols[b_entry, col_at], b_count[b_entry, col_at])
            return summed + term, None

        zero_sum = jnp.zeros((block_rows, BLOCK, block_cols, BLOCK), jnp.float32)
        summed, _ = lax.scan(add_term, zero_sum, jnp.arange(grid_cols, dtype=jnp.int32))
        own_entry = (col_at - row_at) % grid_cols
        own_tile = own_dense(a_vals[row_at, own_entry], a_cols[row_at, own_entry], a_count[row_at, own_entry], block_cols)
        result = 1.5 * own_tile - 0.5 * summed
        return result.astype(jnp.bfloat16).reshape(block_rows * BLOCK, block_cols * BLOCK)

    tiles = lax.map(one_tile, jnp.arange(grid_rows * grid_cols, dtype=jnp.int32))
    tiles = tiles.reshape(grid_rows, grid_cols, block_rows * BLOCK, block_cols * BLOCK)
    return tiles.transpose(0, 2, 1, 3).reshape(grid_rows * block_rows * BLOCK, grid_cols * block_cols * BLOCK)
```

```python
import functools

import jax
import jax.numpy as jnp
from jax import lax
from jax.experimental import pallas as pl
from jax.experimental.pallas import tpu as pltpu
from jax.sharding import PartitionSpec as P

BLOCK = 96
LANES = 128
ROWS = 4
SLOTS_X = 5
COLS = 8
SLOTS_S = 2
WIDE_X = ROWS * BLOCK // LANES
WIDE_S = COLS * BLOCK // LANES
DATA_X = WIDE_X * SLOTS_X * BLOCK
DATA_S = WIDE_S * SLOTS_S * BLOCK
META = 16
WIRE_X = DATA_X + META
WIRE_S = DATA_S + META
HALF_S = 592
MESH = pl.DeviceIdType.MESH
NEAR = (0, 1, -1, 2, -2, 3, -3, 4)
AROUND = (0, 1, 3, 2)


def s_slot(other, dy):
    return 8 * other + NEAR.index(4 if dy == -4 else dy)


def x_slot(other, dx, sibling):
    return 8 * other + 2 * AROUND.index(dx % 4) + sibling


def nt(left, right):
    return lax.dot_general(
        left, right, (((1,), (1,)), ((), ())), preferred_element_type=jnp.float32
    )


def kernel(
    a_cols, a_count, b_cols, b_count, x_in, s_in, out_ref,
    x_tiles, s_tiles, x_dense, s_dense, total, meta, x_recv, s_recv, sent,
):
    row, col = lax.axis_index("row"), lax.axis_index("col")
    y, z_lo = row % 8, row // 8
    core, z_hi, x = col % 2, (col // 2) % 2, col // 4
    parity = z_lo % 2

    def at(x_at, y_at, z_lo_at, z_hi_at, core_at):
        return (z_lo_at * 8 + y_at, (x_at * 2 + z_hi_at) * 2 + core_at)

    def along_x(d):
        return at((x + d + 4) % 4, y, z_lo, z_hi, core)

    def along_y(d):
        return at(x, (y + d + 8) % 8, z_lo, z_hi, core)

    pair_chip = at(x, y, z_lo + 1 - 2 * parity, z_hi, core)
    far_chip = at(x, y, z_lo, 1 - z_hi, core)
    sibling = at(x, y, z_lo, z_hi, 1 - core)
    partners = (
        along_x(1), along_x(-1), along_x(2), along_y(1), along_y(-1), pair_chip, far_chip, sibling
    )
    barrier = pltpu.get_barrier_semaphore()
    for partner in partners:
        pl.semaphore_signal(barrier, inc=1, device_id=partner, device_id_type=MESH)

    sends = []

    def s_part(slot, part):
        if part is None:
            return s_tiles.at[slot]
        start, size = ((0, HALF_S), (HALF_S, WIRE_S - HALF_S))[part]
        return s_tiles.at[slot, pl.ds(start, size)]

    def x_part(slot):
        return x_tiles.at[slot]

    def s_copy(source, target, device, part=None):
        copy = pltpu.make_async_remote_copy(
            src_ref=s_part(source, part), dst_ref=s_part(target, part),
            send_sem=sent.at[len(sends)], recv_sem=s_recv.at[target, part or 0],
            device_id=device, device_id_type=MESH,
        )
        sends.append(functools.partial(s_part, source, part))
        copy.start()

    def x_copy(source, target, device):
        copy = pltpu.make_async_remote_copy(
            src_ref=x_tiles.at[source], dst_ref=x_tiles.at[target],
            send_sem=sent.at[len(sends)], recv_sem=x_recv.at[target],
            device_id=device, device_id_type=MESH,
        )
        sends.append(functools.partial(x_part, source))
        copy.start()

    def s_wait(slot, part=None):
        ref = s_part(slot, part)
        pltpu.make_async_remote_copy(
            src_ref=ref, dst_ref=ref, send_sem=sent.at[0], recv_sem=s_recv.at[slot, part or 0],
            device_id=sibling, device_id_type=MESH,
        ).wait_recv()

    def x_wait(slot):
        ref = x_tiles.at[slot]
        pltpu.make_async_remote_copy(
            src_ref=ref, dst_ref=ref, send_sem=sent.at[0], recv_sem=x_recv.at[slot],
            device_id=sibling, device_id_type=MESH,
        ).wait_recv()

    lane = lax.broadcasted_iota(jnp.int32, (1, LANES), 1)
    unit = (
        lax.broadcasted_iota(jnp.int32, (BLOCK, BLOCK), 0)
        == lax.broadcasted_iota(jnp.int32, (BLOCK, BLOCK), 1)
    ).astype(jnp.bfloat16)

    def lane_columns(where, number, wide, slot):
        first = wide * LANES // BLOCK
        values = []
        for block in (first, first + 1):
            live = slot < number[block]
            values.append(jnp.where(live, where[block, slot], -1).astype(jnp.float32))
        return jnp.where(lane + wide * LANES < (first + 1) * BLOCK, values[0], values[1])

    meta[...] = jnp.full_like(meta, -1.0)
    for wide in range(WIDE_S):
        for slot in range(SLOTS_S):
            index = wide * SLOTS_S + slot
            meta[index : index + 1, :] = lane_columns(b_cols, b_count, wide, slot)
    s_tiles[0, DATA_S:, :] = meta[...].astype(jnp.bfloat16)
    for slot in range(SLOTS_S):
        turned = nt(unit, s_in[slot]).astype(jnp.bfloat16)
        for wide in range(WIDE_S):
            index = wide * SLOTS_S + slot
            s_tiles[0, index * BLOCK : (index + 1) * BLOCK, :] = turned[
                :, wide * LANES : (wide + 1) * LANES
            ]
    pl.semaphore_wait(barrier, len(partners))
    s_copy(0, s_slot(0, -1), along_y(1))
    s_copy(0, s_slot(0, 1), along_y(-1))

    meta[...] = jnp.full_like(meta, -1.0)
    for wide in range(WIDE_X):
        for slot in range(SLOTS_X):
            index = wide * SLOTS_X + slot
            meta[index : index + 1, :] = lane_columns(a_cols, a_count, wide, slot)
    x_tiles[0, DATA_X:, :] = meta[...].astype(jnp.bfloat16)
    for slot in range(SLOTS_X):
        turned = nt(unit, x_in[slot]).astype(jnp.bfloat16)
        for wide in range(WIDE_X):
            index = wide * SLOTS_X + slot
            x_tiles[0, index * BLOCK : (index + 1) * BLOCK, :] = turned[
                :, wide * LANES : (wide + 1) * LANES
            ]
    x_copy(0, x_slot(1, 0, 0), far_chip)
    for d in (1, -1, 2):
        x_copy(0, x_slot(0, -d, 0), along_x(d))
    x_copy(0, x_slot(0, 0, 1), sibling)
    s_copy(0, s_slot(1, 0), pair_chip)
    total[...] = jnp.zeros_like(total)

    def s_ring(other, near):
        for sign in (1, -1):
            here = s_slot(other, sign * near)
            s_wait(here)
            s_copy(here, s_slot(other, sign * (near + 1)), along_y(-sign))

    def x_share(other, dx):
        x_wait(x_slot(other, dx, 0))
        x_copy(x_slot(other, dx, 0), x_slot(other, dx, 1), sibling)

    def step_1():
        s_ring(0, 1)
        x_wait(x_slot(0, 0, 1))

    def step_2():
        x_share(0, 1)
        x_share(0, -1)

    def step_3():
        s_ring(0, 2)
        x_wait(x_slot(0, 1, 1))

    def step_4():
        here = x_slot(1, 0, 0)
        x_wait(here)
        for d in (1, -1, 2):
            x_copy(here, x_slot(1, -d, 0), along_x(d))
        x_copy(here, x_slot(1, 0, 1), sibling)

    def step_5():
        s_wait(s_slot(0, 3))
        s_copy(s_slot(0, 3), s_slot(0, 4), along_y(-1), 1)
        s_wait(s_slot(0, -3))
        s_copy(s_slot(0, -3), s_slot(0, 4), along_y(1), 0)
        s_wait(s_slot(1, 0))
        s_copy(s_slot(1, 0), s_slot(1, 1), along_y(-1))
        s_copy(s_slot(1, 0), s_slot(1, -1), along_y(1))
        for sign in (1, -1):
            s_copy(s_slot(0, sign * 3), s_slot(1, sign * 3), pair_chip, 0)
        x_wait(x_slot(0, -1, 1))

    def step_6():
        x_share(0, 2)

    def step_7():
        for part in (0, 1):
            s_wait(s_slot(0, 4), part)
        s_copy(s_slot(0, 4), s_slot(1, 4), pair_chip)
        x_wait(x_slot(0, 2, 1))

    def step_9():
        s_ring(1, 1)
        x_wait(x_slot(1, 0, 1))

    def step_10():
        x_share(1, 1)
        x_share(1, -1)

    def step_11():
        for sign in (1, -1):
            here = s_slot(1, sign * 2)
            s_wait(here)
            s_copy(here, s_slot(1, sign * 3), along_y(-sign), 1)
        x_wait(x_slot(1, 1, 1))

    def step_13():
        for sign in (1, -1):
            for part in (0, 1):
                s_wait(s_slot(1, sign * 3), part)
        x_wait(x_slot(1, -1, 1))

    def step_14():
        x_share(1, 2)

    def step_15():
        s_wait(s_slot(1, 4))
        x_wait(x_slot(1, 2, 1))

    events = {
        1: step_1, 2: step_2, 3: step_3, 4: step_4, 5: step_5, 6: step_6, 7: step_7, 9: step_9,
        10: step_10, 11: step_11, 13: step_13, 14: step_14, 15: step_15,
    }

    def x_for_s(s_at):
        h = s_at % 8
        dy = ((h + 1) // 2) * (2 * (h % 2) - 1)
        other = s_at // 8
        u = ((parity + other) % 2) * 8 + (y + dy + 8) % 8
        t = (u + col - row + 32) % 16
        dx = (t // 4 - x + 4) % 4
        place = jnp.where(dx == 3, 2, jnp.where(dx == 2, 3, dx))
        far = ((t // 2) % 2 + z_hi) % 2
        return far * 8 + place * 2 + (t % 2 + core) % 2

    def s_for_x(x_at):
        place = (x_at // 2) % 4
        dx = jnp.where(place == 3, 2, jnp.where(place == 2, 3, place))
        t = ((x + dx) % 4) * 4 + ((z_hi + x_at // 8) % 2) * 2 + (core + x_at) % 2
        u = (t + row - col + 16) % 16
        dy = (u % 8 - y + 8) % 8
        h = jnp.where(dy == 0, 0, jnp.where(dy <= 4, 2 * dy - 1, 2 * (8 - dy)))
        return ((u // 8 + parity) % 2) * 8 + h

    def multiply(s_at, x_at):
        names = x_tiles[x_at, DATA_X:, :]
        for wide in range(WIDE_X):
            stored, column = [], []
            for slot in range(SLOTS_X):
                index = wide * SLOTS_X + slot
                stored.append(x_tiles[x_at, index * BLOCK : (index + 1) * BLOCK, :])
                column.append(jnp.broadcast_to(names[index : index + 1, :], (BLOCK, LANES)))
            for j in range(COLS):
                placed = jnp.zeros((BLOCK, LANES), jnp.bfloat16)
                for slot in range(SLOTS_X):
                    placed = jnp.where(column[slot] == j, stored[slot], placed)
                x_dense[j * BLOCK : (j + 1) * BLOCK, wide * LANES : (wide + 1) * LANES] = placed
        names = s_tiles[s_at, DATA_S:, :]
        for wide in range(WIDE_S):
            stored, column = [], []
            for slot in range(SLOTS_S):
                index = wide * SLOTS_S + slot
                stored.append(s_tiles[s_at, index * BLOCK : (index + 1) * BLOCK, :])
                column.append(jnp.broadcast_to(names[index : index + 1, :], (BLOCK, LANES)))
            for j in range(COLS):
                placed = jnp.zeros((BLOCK, LANES), jnp.bfloat16)
                for slot in range(SLOTS_S):
                    placed = jnp.where(column[slot] == j, stored[slot], placed)
                s_dense[j * BLOCK : (j + 1) * BLOCK, wide * LANES : (wide + 1) * LANES] = placed
        total[...] += jnp.dot(s_dense[...], x_dense[...], preferred_element_type=jnp.float32)

        own = (s_at // 8 + parity) % 2 * 8
        h = s_at % 8
        dy = ((h + 1) // 2) * (2 * (h % 2) - 1)

        @pl.when(own + (y + dy + 8) % 8 == 0)
        def _():
            total[...] -= 3.0 * x_dense[...].astype(jnp.float32)

    def body(step, carry):
        place = step // 2
        by_x = step % 2
        for at_place, event in events.items():
            pl.when(step == 2 * at_place)(event)
        s_at = jnp.where(by_x == 1, s_for_x(place), place)
        x_at = jnp.where(by_x == 1, place, x_for_s(place))
        ready = jnp.where(by_x == 1, s_at < place, x_at <= place)

        @pl.when(ready)
        def _():
            multiply(s_at, x_at)

        return carry

    lax.fori_loop(0, 32, body, 0)
    out_ref[...] = (-0.5 * total[...]).astype(jnp.bfloat16)
    assert len(sends) == N_SENDS
    for index, part in enumerate(sends):
        pltpu.make_async_remote_copy(
            src_ref=part(), dst_ref=part(), send_sem=sent.at[index], recv_sem=x_recv.at[0],
            device_id=sibling, device_id_type=MESH,
        ).wait_send()


N_SENDS = 33


def shards(a_vals, a_cols, a_count, b_vals, b_cols, b_count):
    x_in = a_vals.reshape(ROWS, SLOTS_X, BLOCK, BLOCK).transpose(1, 0, 2, 3)
    x_in = x_in.reshape(SLOTS_X, ROWS * BLOCK, BLOCK)
    s_in = b_vals.reshape(COLS, SLOTS_S, BLOCK, BLOCK).transpose(1, 0, 2, 3)
    s_in = s_in.reshape(SLOTS_S, COLS * BLOCK, BLOCK)
    scalars = pl.BlockSpec(memory_space=pltpu.SMEM)
    blocks = pl.BlockSpec(memory_space=pltpu.VMEM)
    turned = pl.pallas_call(
        kernel,
        out_shape=jax.ShapeDtypeStruct((COLS * BLOCK, ROWS * BLOCK), jnp.bfloat16),
        in_specs=[scalars] * 4 + [blocks] * 2,
        out_specs=blocks,
        scratch_shapes=[
            pltpu.VMEM((16, WIRE_X, LANES), jnp.bfloat16),
            pltpu.VMEM((16, WIRE_S, LANES), jnp.bfloat16),
            pltpu.VMEM((COLS * BLOCK, ROWS * BLOCK), jnp.bfloat16),
            pltpu.VMEM((COLS * BLOCK, COLS * BLOCK), jnp.bfloat16),
            pltpu.VMEM((COLS * BLOCK, ROWS * BLOCK), jnp.float32),
            pltpu.VMEM((META, LANES), jnp.float32),
            pltpu.SemaphoreType.DMA((16,)),
            pltpu.SemaphoreType.DMA((16, 2)),
            pltpu.SemaphoreType.DMA((N_SENDS,)),
        ],
        compiler_params=pltpu.CompilerParams(
            collective_id=0, has_side_effects=True, vmem_limit_bytes=40 * 1024 * 1024
        ),
        name="gather_multiply",
    )(a_cols[0, 0], a_count[0, 0], b_cols[0, 0], b_count[0, 0], x_in, s_in)
    return turned.T


def solution(mesh):
    in_specs = (
        P("row", "col", None, None, None),
        P("row", "col", None, None),
        P("row", "col", None),
        P("row", "col", None, None, None),
        P("row", "col", None, None),
        P("row", "col", None),
    )
    out_specs = P("row", "col")
    return jax.shard_map(shards, mesh=mesh, in_specs=in_specs, out_specs=out_specs, check_vma=False)
```

```python
import functools

import jax
import jax.numpy as jnp
from jax import lax
from jax.experimental import pallas as pl
from jax.experimental.pallas import tpu as pltpu
from jax.sharding import PartitionSpec as P

BLOCK = 96
LANES = 128
ROWS = 4
SLOTS_X = 5
COLS = 8
SLOTS_S = 2
WIDE_X = ROWS * BLOCK // LANES
WIDE_S = COLS * BLOCK // LANES
DATA_X = WIDE_X * SLOTS_X * BLOCK
DATA_S = WIDE_S * SLOTS_S * BLOCK
META = 16
WIRE_X = DATA_X + META
WIRE_S = DATA_S + META
SPLIT_X = (0, 720, WIRE_X)
SPLIT_S = (0, 576, WIRE_S)
MESH = pl.DeviceIdType.MESH
AROUND = (0, 1, 3, 2)
HALVES = (0, 1)
OWN = {0: 0, 1: 1, -1: 2, 2: 3, -2: 4, 3: 5, -3: 6, 4: 7}
OTHER = {0: 8, 1: 9, -1: 10, 2: 12, -2: 13, 4: 14}
BY_PAIR, BY_RING = 11, 15


def x_slot(other, dx, sibling=0):
    return 8 * other + 2 * AROUND.index(dx % 4) + sibling


def nt(left, right):
    return lax.dot_general(
        left, right, (((1,), (1,)), ((), ())), preferred_element_type=jnp.float32
    )


def kernel(
    a_cols, a_count, b_cols, b_count, x_in, s_in, out_ref,
    x_tiles, s_tiles, x_dense, s_dense, total, meta, x_recv, s_recv, sent,
):
    row, col = lax.axis_index("row"), lax.axis_index("col")
    y, z_lo = row % 8, row // 8
    core, z_hi, x = col % 2, (col // 2) % 2, col // 4
    parity = z_lo % 2

    def at(x_at, y_at, z_lo_at, z_hi_at, core_at):
        return (z_lo_at * 8 + y_at, (x_at * 2 + z_hi_at) * 2 + core_at)

    def along_x(d):
        return at((x + d + 4) % 4, y, z_lo, z_hi, core)

    def along_y(d):
        return at(x, (y + d + 8) % 8, z_lo, z_hi, core)

    pair_chip = at(x, y, z_lo + 1 - 2 * parity, z_hi, core)
    far_chip = at(x, y, z_lo, 1 - z_hi, core)
    sibling = at(x, y, z_lo, z_hi, 1 - core)
    near_chips = (along_x(1), along_x(-1), along_y(1), along_y(-1), pair_chip, sibling)
    barrier = pltpu.get_barrier_semaphore()

    def greet(device):
        pl.semaphore_signal(barrier, inc=1, device_id=device, device_id_type=MESH)

    for device in near_chips:
        greet(device)

    sends = []

    def s_part(slot, half):
        start = SPLIT_S[half]
        return s_tiles.at[slot, pl.ds(start, SPLIT_S[half + 1] - start)]

    def x_part(slot, half):
        start = SPLIT_X[half]
        return x_tiles.at[slot, pl.ds(start, SPLIT_X[half + 1] - start)]

    def send(part, arrived, source, target, device, half, index=None):
        if index is None:
            index = len(sends)
            sends.append(functools.partial(part, source, half))
        pltpu.make_async_remote_copy(
            src_ref=part(source, half), dst_ref=part(target, half),
            send_sem=sent.at[index], recv_sem=arrived.at[target, half],
            device_id=device, device_id_type=MESH,
        ).start()

    def wait(part, arrived, slot, half):
        ref = part(slot, half)
        pltpu.make_async_remote_copy(
            src_ref=ref, dst_ref=ref, send_sem=sent.at[0], recv_sem=arrived.at[slot, half],
            device_id=sibling, device_id_type=MESH,
        ).wait_recv()

    s_copy = functools.partial(send, s_part, s_recv)
    x_copy = functools.partial(send, x_part, x_recv)
    s_wait = functools.partial(wait, s_part, s_recv)
    x_wait = functools.partial(wait, x_part, x_recv)

    lane = lax.broadcasted_iota(jnp.int32, (1, LANES), 1)
    unit = (
        lax.broadcasted_iota(jnp.int32, (BLOCK, BLOCK), 0)
        == lax.broadcasted_iota(jnp.int32, (BLOCK, BLOCK), 1)
    ).astype(jnp.bfloat16)

    def lane_columns(where, number, wide, slot):
        first = wide * LANES // BLOCK
        values = []
        for block in (first, first + 1):
            live = slot < number[block]
            values.append(jnp.where(live, where[block, slot], -1).astype(jnp.float32))
        return jnp.where(lane + wide * LANES < (first + 1) * BLOCK, values[0], values[1])

    meta[...] = jnp.full_like(meta, -1.0)
    for wide in range(WIDE_S):
        for slot in range(SLOTS_S):
            index = wide * SLOTS_S + slot
            meta[index : index + 1, :] = lane_columns(b_cols, b_count, wide, slot)
    s_tiles[0, DATA_S:, :] = meta[...].astype(jnp.bfloat16)
    for slot in range(SLOTS_S):
        turned = nt(unit, s_in[slot]).astype(jnp.bfloat16)
        for wide in range(WIDE_S):
            index = wide * SLOTS_S + slot
            s_tiles[0, index * BLOCK : (index + 1) * BLOCK, :] = turned[
                :, wide * LANES : (wide + 1) * LANES
            ]
    pl.semaphore_wait(barrier, len(near_chips) + z_hi)
    greet(far_chip)
    for half in HALVES:
        s_copy(0, OWN[-1], along_y(1), half)
        s_copy(0, OWN[1], along_y(-1), half)

    meta[...] = jnp.full_like(meta, -1.0)
    for wide in range(WIDE_X):
        for slot in range(SLOTS_X):
            index = wide * SLOTS_X + slot
            meta[index : index + 1, :] = lane_columns(a_cols, a_count, wide, slot)
    x_tiles[0, DATA_X:, :] = meta[...].astype(jnp.bfloat16)
    for slot in range(SLOTS_X):
        turned = nt(unit, x_in[slot]).astype(jnp.bfloat16)
        for wide in range(WIDE_X):
            index = wide * SLOTS_X + slot
            x_tiles[0, index * BLOCK : (index + 1) * BLOCK, :] = turned[
                :, wide * LANES : (wide + 1) * LANES
            ]
    far_sends = len(sends)
    sends.extend(functools.partial(x_part, 0, half) for half in HALVES)

    def x_leave():
        for half in HALVES:
            x_copy(0, x_slot(1, 0), far_chip, half, far_sends + half)

    def x_leave_late():
        @pl.when(z_hi == 0)
        def _():
            pl.semaphore_wait(barrier, 1)
            x_leave()

    pl.when(z_hi == 1)(x_leave)
    for half in HALVES:
        x_copy(0, x_slot(0, -1), along_x(1), half)
        x_copy(0, x_slot(0, 1), along_x(-1), half)
    for half in HALVES:
        x_copy(0, x_slot(0, 0, 1), sibling, half)
    for half in HALVES:
        s_copy(0, OTHER[0], pair_chip, half)
    total[...] = jnp.zeros_like(total)

    def s_ring(slots, near, half):
        for sign in (1, -1):
            here = slots[sign * near]
            s_wait(here, half)
            s_copy(here, slots[sign * (near + 1)], along_y(-sign), half)

    def x_near(other):
        for half in HALVES:
            for d in (1, -1):
                here = x_slot(other, d)
                x_wait(here, half)
                if (half == 0) == (d == 1):
                    x_copy(here, x_slot(other, 2), along_x(-d), half)
                x_copy(here, here + 1, sibling, half)

    def x_across(other):
        here = x_slot(other, 2)
        for half in HALVES:
            x_wait(here, half)
            x_copy(here, here + 1, sibling, half)

    def x_far(half):
        here = x_slot(1, 0)
        x_wait(here, half)
        x_copy(here, x_slot(1, -1), along_x(1), half)
        x_copy(here, x_slot(1, 1), along_x(-1), half)
        x_copy(here, here + 1, sibling, half)

    def x_sibling(other, dx):
        for half in HALVES:
            x_wait(x_slot(other, dx, 1), half)

    pair_third = OWN[-3] - core
    ring_second, other_second = OTHER[2] + core, OTHER[-2] - core
    ring_chip = along_y(2 * core - 1)

    def s_third_first():
        s_wait(OWN[3], 0)
        s_copy(OWN[3], OWN[4], along_y(-1), 0)
        s_wait(OWN[-3], 0)
        s_copy(pair_third, BY_PAIR, pair_chip, 0)

    def s_third_last():
        s_wait(OWN[-3], 1)
        s_copy(OWN[-3], OWN[4], along_y(1), 1)
        s_wait(OWN[3], 1)
        s_copy(pair_third, BY_PAIR, pair_chip, 1)

    def s_other_start():
        for half in HALVES:
            s_wait(OTHER[0], half)
            s_copy(OTHER[0], OTHER[1], along_y(-1), half)
            s_copy(OTHER[0], OTHER[-1], along_y(1), half)

    def s_fourth():
        for half in HALVES:
            s_wait(OWN[4], half)
            s_copy(OWN[4], OTHER[4], pair_chip, half)

    def s_other_second():
        for half in HALVES:
            s_wait(ring_second, half)
            s_copy(ring_second, BY_RING, ring_chip, half)
        for half in HALVES:
            s_wait(other_second, half)

    def s_last(slot):
        for half in HALVES:
            s_wait(slot, half)

    part = functools.partial
    plan = (
        "S", "X",
        part(s_ring, OWN, 1, 0), part(x_sibling, 0, 0), "X",
        part(s_ring, OWN, 1, 1), x_leave_late, "S", "S",
        part(s_ring, OWN, 2, 0), part(x_far, 0), part(x_near, 0), "X",
        part(s_ring, OWN, 2, 1), "S", "S",
        part(x_sibling, 0, 1), "X", "X", part(x_sibling, 0, -1), "X",
        s_third_first, part(x_far, 1), s_third_last, "S", "S",
        s_other_start, part(x_across, 0), "X", part(x_sibling, 0, 2), "X",
        s_fourth, "S", "S",
        "X", part(x_sibling, 1, 0), "X",
        part(s_ring, OTHER, 1, 0), part(x_near, 1), "X", part(x_sibling, 1, 1), "X",
        part(s_ring, OTHER, 1, 1), "S", "S",
        "X", part(x_sibling, 1, -1), "X", part(x_across, 1), "X", part(x_sibling, 1, 2), "X",
        part(s_last, BY_PAIR), "S",
        s_other_second, "S", "S",
        part(s_last, OTHER[4]), "S",
        part(s_last, BY_RING), "S",
    )
    events, turns, bits = {}, 0, 0
    for entry in plan:
        if entry in ("S", "X"):
            bits += (entry == "X") << turns
            turns += 1
        else:
            events.setdefault(turns, []).append(entry)
    low_bits, high_bits = bits % 2**16, bits // 2**16
    third = 3 - 6 * core

    def distance(s_at):
        h = s_at % 8
        own = ((h + 1) // 2) * (2 * (h % 2) - 1)
        tail = jnp.where(h == 3, -third, jnp.where(h == 7, third, jnp.where(h == 6, 4, 18 - 4 * h)))
        return jnp.where((s_at >= 8) & (h >= 3), tail, own)

    def s_row(s_at):
        return (parity + s_at // 8) % 2 * 8 + (y + distance(s_at) + 8) % 8

    def x_for_s(s_at):
        t = (s_row(s_at) + col - row + 32) % 16
        dx = (t // 4 - x + 4) % 4
        place = jnp.where(dx == 3, 2, jnp.where(dx == 2, 3, dx))
        far = ((t // 2) % 2 + z_hi) % 2
        return far * 8 + place * 2 + (t % 2 + core) % 2

    def s_for_x(x_at):
        place = (x_at // 2) % 4
        dx = jnp.where(place == 3, 2, jnp.where(place == 2, 3, place))
        t = ((x + dx) % 4) * 4 + ((z_hi + x_at // 8) % 2) * 2 + (core + x_at) % 2
        u = (t + row - col + 16) % 16
        dy = (u % 8 - y + 8) % 8
        dy = jnp.where(dy > 4, dy - 8, dy)
        own = jnp.where(dy > 0, 2 * dy - 1, -2 * dy)
        tail = jnp.where(dy == third, 7, jnp.where(dy == -third, 3, jnp.where(dy == 4, 6, own + 1)))
        tail = jnp.where(own < 3, own, tail)
        return jnp.where((u // 8 + parity) % 2 == 1, 8 + tail, own)

    def multiply(s_at, x_at):
        names = x_tiles[x_at, DATA_X:, :]
        for wide in range(WIDE_X):
            stored, column = [], []
            for slot in range(SLOTS_X):
                index = wide * SLOTS_X + slot
                stored.append(x_tiles[x_at, index * BLOCK : (index + 1) * BLOCK, :])
                column.append(jnp.broadcast_to(names[index : index + 1, :], (BLOCK, LANES)))
            for j in range(COLS):
                placed = jnp.zeros((BLOCK, LANES), jnp.bfloat16)
                for slot in range(SLOTS_X):
                    placed = jnp.where(column[slot] == j, stored[slot], placed)
                x_dense[j * BLOCK : (j + 1) * BLOCK, wide * LANES : (wide + 1) * LANES] = placed
        names = s_tiles[s_at, DATA_S:, :]
        for wide in range(WIDE_S):
            stored, column = [], []
            for slot in range(SLOTS_S):
                index = wide * SLOTS_S + slot
                stored.append(s_tiles[s_at, index * BLOCK : (index + 1) * BLOCK, :])
                column.append(jnp.broadcast_to(names[index : index + 1, :], (BLOCK, LANES)))
            for j in range(COLS):
                placed = jnp.zeros((BLOCK, LANES), jnp.bfloat16)
                for slot in range(SLOTS_S):
                    placed = jnp.where(column[slot] == j, stored[slot], placed)
                s_dense[j * BLOCK : (j + 1) * BLOCK, wide * LANES : (wide + 1) * LANES] = placed
        total[...] += jnp.dot(s_dense[...], x_dense[...], preferred_element_type=jnp.float32)

        @pl.when(s_row(s_at) == 0)
        def _():
            total[...] -= 3.0 * x_dense[...].astype(jnp.float32)

    def body(step, arrived):
        s_count, x_count = arrived
        for turn, entries in events.items():

            @pl.when(step == turn)
            def _():
                for entry in entries:
                    entry()

        by_x = (jnp.where(step < 16, low_bits, high_bits) >> (step % 16)) % 2
        s_at = jnp.where(by_x == 1, s_for_x(x_count), s_count)
        x_at = jnp.where(by_x == 1, x_count, x_for_s(s_count))
        ready = jnp.where(by_x == 1, s_at < s_count, x_at < x_count)

        @pl.when(ready)
        def _():
            multiply(s_at, x_at)

        return s_count + 1 - by_x, x_count + by_x

    lax.fori_loop(0, turns, body, (0, 0))
    out_ref[...] = (-0.5 * total[...]).astype(jnp.bfloat16)
    assert len(sends) == N_SENDS, len(sends)
    for index, ref in enumerate(sends):
        pltpu.make_async_remote_copy(
            src_ref=ref(), dst_ref=ref(), send_sem=sent.at[index], recv_sem=x_recv.at[0, 0],
            device_id=sibling, device_id_type=MESH,
        ).wait_send()


N_SENDS = 60


def shards(a_vals, a_cols, a_count, b_vals, b_cols, b_count):
    x_in = a_vals.reshape(ROWS, SLOTS_X, BLOCK, BLOCK).transpose(1, 0, 2, 3)
    x_in = x_in.reshape(SLOTS_X, ROWS * BLOCK, BLOCK)
    s_in = b_vals.reshape(COLS, SLOTS_S, BLOCK, BLOCK).transpose(1, 0, 2, 3)
    s_in = s_in.reshape(SLOTS_S, COLS * BLOCK, BLOCK)
    scalars = pl.BlockSpec(memory_space=pltpu.SMEM)
    blocks = pl.BlockSpec(memory_space=pltpu.VMEM)
    turned = pl.pallas_call(
        kernel,
        out_shape=jax.ShapeDtypeStruct((COLS * BLOCK, ROWS * BLOCK), jnp.bfloat16),
        in_specs=[scalars] * 4 + [blocks] * 2,
        out_specs=blocks,
        scratch_shapes=[
            pltpu.VMEM((16, WIRE_X, LANES), jnp.bfloat16),
            pltpu.VMEM((16, WIRE_S, LANES), jnp.bfloat16),
            pltpu.VMEM((COLS * BLOCK, ROWS * BLOCK), jnp.bfloat16),
            pltpu.VMEM((COLS * BLOCK, COLS * BLOCK), jnp.bfloat16),
            pltpu.VMEM((COLS * BLOCK, ROWS * BLOCK), jnp.float32),
            pltpu.VMEM((META, LANES), jnp.float32),
            pltpu.SemaphoreType.DMA((16, 2)),
            pltpu.SemaphoreType.DMA((16, 2)),
            pltpu.SemaphoreType.DMA((N_SENDS,)),
        ],
        compiler_params=pltpu.CompilerParams(
            collective_id=0, has_side_effects=True, vmem_limit_bytes=40 * 1024 * 1024
        ),
        name="gather_multiply",
    )(a_cols[0, 0], a_count[0, 0], b_cols[0, 0], b_count[0, 0], x_in, s_in)
    return turned.T


def solution(mesh):
    in_specs = (
        P("row", "col", None, None, None),
        P("row", "col", None, None),
        P("row", "col", None),
        P("row", "col", None, None, None),
        P("row", "col", None, None),
        P("row", "col", None),
    )
    out_specs = P("row", "col")
    return jax.shard_map(shards, mesh=mesh, in_specs=in_specs, out_specs=out_specs, check_vma=False)
```

```python
import functools

import jax
import jax.numpy as jnp
from jax import lax
from jax.experimental import pallas as pl
from jax.experimental.pallas import tpu as pltpu
from jax.sharding import PartitionSpec as P

BLOCK = 96
LANES = 128
ROWS = 4
SLOTS_X = 5
COLS = 8
SLOTS_S = 2
WIDE_X = ROWS * BLOCK // LANES
WIDE_S = COLS * BLOCK // LANES
DATA_X = WIDE_X * SLOTS_X * BLOCK
DATA_S = WIDE_S * SLOTS_S * BLOCK
META = 16
WIRE_X = DATA_X + META
WIRE_S = DATA_S + META
SPLIT_X = (0, 720, WIRE_X)
SPLIT_S = (0, 576, WIRE_S)
MESH = pl.DeviceIdType.MESH
AROUND = (0, 1, 3, 2)
HALVES = (0, 1)
OWN = {0: 0, 1: 1, -1: 2, 2: 3, -2: 4, 3: 5, -3: 6, 4: 7}
OTHER = {0: 8, 1: 9, -1: 10, 2: 12, -2: 13, 4: 14}
BY_PAIR, BY_RING = 11, 15


def x_slot(other, dx, sibling=0):
    return 8 * other + 2 * AROUND.index(dx % 4) + sibling


def div(number, by):
    return lax.div(number, jnp.int32(by))


def rem(number, by):
    return lax.rem(number, jnp.int32(by))


def nt(left, right):
    return lax.dot_general(
        left, right, (((1,), (1,)), ((), ())), preferred_element_type=jnp.float32
    )


def kernel(
    a_cols_in, a_count_in, b_cols_in, b_count_in, x_in, s_in, out_ref,
    a_cols, a_count, b_cols, b_count, scalars_came, x_tiles, s_tiles, x_dense, s_dense, total, meta, x_recv, s_recv, sent,
):
    row, col = lax.axis_index("row"), lax.axis_index("col")
    y, z_lo = rem(row, 8), div(row, 8)
    core, z_hi, x = rem(col, 2), rem(div(col, 2), 2), div(col, 4)
    parity = rem(z_lo, 2)

    def at(x_at, y_at, z_lo_at, z_hi_at, core_at):
        return (z_lo_at * 8 + y_at, (x_at * 2 + z_hi_at) * 2 + core_at)

    def along_x(d):
        return at(rem(x + d + 4, 4), y, z_lo, z_hi, core)

    def along_y(d):
        return at(x, rem(y + d + 8, 8), z_lo, z_hi, core)

    pair_chip = at(x, y, z_lo + 1 - 2 * parity, z_hi, core)
    far_chip = at(x, y, z_lo, 1 - z_hi, core)
    sibling = at(x, y, z_lo, z_hi, 1 - core)
    near_chips = (along_x(1), along_x(-1), along_y(1), along_y(-1), pair_chip, sibling)
    barrier = pltpu.get_barrier_semaphore()

    def greet(device):
        pl.semaphore_signal(barrier, inc=1, device_id=device, device_id_type=MESH)

    for device in near_chips:
        greet(device)
    scalars = [
        pltpu.make_async_copy(source, target, scalars_came.at[index])
        for index, (source, target) in enumerate(
            ((a_cols_in, a_cols), (a_count_in, a_count), (b_cols_in, b_cols), (b_count_in, b_count))
        )
    ]
    for copy in scalars:
        copy.start()

    sends = []

    def s_part(slot, half):
        start = SPLIT_S[half]
        return s_tiles.at[slot, pl.ds(start, SPLIT_S[half + 1] - start)]

    def x_part(slot, half):
        start = SPLIT_X[half]
        return x_tiles.at[slot, pl.ds(start, SPLIT_X[half + 1] - start)]

    def send(part, arrived, source, target, device, half, index=None):
        if index is None:
            index = len(sends)
            sends.append(functools.partial(part, source, half))
        pltpu.make_async_remote_copy(
            src_ref=part(source, half), dst_ref=part(target, half),
            send_sem=sent.at[index], recv_sem=arrived.at[target, half],
            device_id=device, device_id_type=MESH,
        ).start()

    def wait(part, arrived, slot, half):
        ref = part(slot, half)
        pltpu.make_async_remote_copy(
            src_ref=ref, dst_ref=ref, send_sem=sent.at[0], recv_sem=arrived.at[slot, half],
            device_id=sibling, device_id_type=MESH,
        ).wait_recv()

    s_copy = functools.partial(send, s_part, s_recv)
    x_copy = functools.partial(send, x_part, x_recv)
    s_wait = functools.partial(wait, s_part, s_recv)
    x_wait = functools.partial(wait, x_part, x_recv)

    lane = lax.broadcasted_iota(jnp.int32, (1, LANES), 1)
    unit = (
        lax.broadcasted_iota(jnp.int32, (BLOCK, BLOCK), 0)
        == lax.broadcasted_iota(jnp.int32, (BLOCK, BLOCK), 1)
    ).astype(jnp.bfloat16)

    def lane_columns(where, number, wide, slot):
        first = wide * LANES // BLOCK
        values = []
        for block in (first, first + 1):
            live = slot < number[block]
            values.append(jnp.where(live, where(block, slot), -1).astype(jnp.float32))
        return jnp.where(lane + wide * LANES < (first + 1) * BLOCK, values[0], values[1])

    for copy in scalars:
        copy.wait()
    meta[...] = jnp.full_like(meta, -1.0)
    for wide in range(WIDE_S):
        for slot in range(SLOTS_S):
            index = wide * SLOTS_S + slot
            meta[index : index + 1, :] = lane_columns(lambda block, slot: b_cols[slot, block], b_count, wide, slot)
    s_tiles[0, DATA_S:, :] = meta[...].astype(jnp.bfloat16)
    for slot in range(SLOTS_S):
        turned = nt(unit, s_in[slot]).astype(jnp.bfloat16)
        for wide in range(WIDE_S):
            index = wide * SLOTS_S + slot
            s_tiles[0, index * BLOCK : (index + 1) * BLOCK, :] = turned[
                :, wide * LANES : (wide + 1) * LANES
            ]
    pl.semaphore_wait(barrier, len(near_chips) + z_hi)
    greet(far_chip)
    for half in HALVES:
        s_copy(0, OWN[-1], along_y(1), half)
        s_copy(0, OWN[1], along_y(-1), half)

    meta[...] = jnp.full_like(meta, -1.0)
    for wide in range(WIDE_X):
        for slot in range(SLOTS_X):
            index = wide * SLOTS_X + slot
            meta[index : index + 1, :] = lane_columns(lambda block, slot: a_cols[block, slot], a_count, wide, slot)
    x_tiles[0, DATA_X:, :] = meta[...].astype(jnp.bfloat16)
    for slot in range(SLOTS_X):
        turned = nt(unit, x_in[slot]).astype(jnp.bfloat16)
        for wide in range(WIDE_X):
            index = wide * SLOTS_X + slot
            x_tiles[0, index * BLOCK : (index + 1) * BLOCK, :] = turned[
                :, wide * LANES : (wide + 1) * LANES
            ]
    far_sends = len(sends)
    sends.extend(functools.partial(x_part, 0, half) for half in HALVES)

    def x_leave():
        for half in HALVES:
            x_copy(0, x_slot(1, 0), far_chip, half, far_sends + half)

    def x_leave_late():
        @pl.when(z_hi == 0)
        def _():
            pl.semaphore_wait(barrier, 1)
            x_leave()

    pl.when(z_hi == 1)(x_leave)
    for half in HALVES:
        x_copy(0, x_slot(0, -1), along_x(1), half)
        x_copy(0, x_slot(0, 1), along_x(-1), half)
    for half in HALVES:
        x_copy(0, x_slot(0, 0, 1), sibling, half)
    for half in HALVES:
        s_copy(0, OTHER[0], pair_chip, half)
    total[...] = jnp.zeros_like(total)

    def s_ring(slots, near, half):
        for sign in (1, -1):
            here = slots[sign * near]
            s_wait(here, half)
            s_copy(here, slots[sign * (near + 1)], along_y(-sign), half)

    def x_near(other, half):
        for d in (1, -1):
            here = x_slot(other, d)
            x_wait(here, half)
            if (half == 0) == (d == 1):
                x_copy(here, x_slot(other, 2), along_x(-d), half)
            x_copy(here, here + 1, sibling, half)

    def x_across(other):
        here = x_slot(other, 2)
        for half in HALVES:
            x_wait(here, half)
            x_copy(here, here + 1, sibling, half)

    def x_far(half):
        here = x_slot(1, 0)
        x_wait(here, half)
        x_copy(here, x_slot(1, -1), along_x(1), half)
        x_copy(here, x_slot(1, 1), along_x(-1), half)
        x_copy(here, here + 1, sibling, half)

    def x_sibling(other, dx):
        for half in HALVES:
            x_wait(x_slot(other, dx, 1), half)

    pair_third = OWN[-3] - core
    ring_second, other_second = OTHER[2] + core, OTHER[-2] - core
    ring_chip = along_y(2 * core - 1)

    def s_third_first():
        s_wait(OWN[3], 0)
        s_copy(OWN[3], OWN[4], along_y(-1), 0)
        s_wait(OWN[-3], 0)
        s_copy(pair_third, BY_PAIR, pair_chip, 0)

    def s_third_last():
        s_wait(OWN[-3], 1)
        s_copy(OWN[-3], OWN[4], along_y(1), 1)
        s_wait(OWN[3], 1)
        s_copy(pair_third, BY_PAIR, pair_chip, 1)

    def s_other_start():
        for half in HALVES:
            s_wait(OTHER[0], half)
            s_copy(OTHER[0], OTHER[1], along_y(-1), half)
            s_copy(OTHER[0], OTHER[-1], along_y(1), half)

    def s_fourth():
        for half in HALVES:
            s_wait(OWN[4], half)
            s_copy(OWN[4], OTHER[4], pair_chip, half)

    def s_other_second(half):
        s_wait(ring_second, half)
        s_copy(ring_second, BY_RING, ring_chip, half)

    def s_last(slot):
        for half in HALVES:
            s_wait(slot, half)

    part = functools.partial
    plan = (
        "S", "X",
        part(s_ring, OWN, 1, 0), part(x_sibling, 0, 0), "X",
        part(s_ring, OWN, 1, 1), x_leave_late, "S", "S",
        part(s_ring, OWN, 2, 0), part(x_near, 0, 0), part(x_near, 0, 1), "X",
        part(s_ring, OWN, 2, 1), "S", "S",
        part(x_sibling, 0, 1), "X", "X",
        s_third_first, part(x_sibling, 0, -1), "X", part(x_across, 0), s_third_last, part(x_far, 0), "S", "S",
        s_other_start, "X", part(x_sibling, 0, 2), "X",
        s_fourth, part(x_far, 1), "S", "S",
        "X", part(s_ring, OTHER, 1, 0), part(x_near, 1, 0), part(x_sibling, 1, 0), "X",
        part(s_ring, OTHER, 1, 1), part(x_near, 1, 1), "S", "S", "X",
        part(s_other_second, 0), part(x_sibling, 1, 1), "X", "X", part(s_last, BY_PAIR), "S",
        part(s_other_second, 1), part(x_sibling, 1, -1), "X", part(x_across, 1),
        part(s_last, other_second), "S", "S", "X",
        part(s_last, OTHER[4]), "S",
        part(x_sibling, 1, 2), "X",
        part(s_last, BY_RING), "S",
    )
    events, turns, bits = {}, 0, 0
    for entry in plan:
        if entry in ("S", "X"):
            bits += (entry == "X") << turns
            turns += 1
        else:
            events.setdefault(turns, []).append(entry)
    low_bits, high_bits = bits % 2**16, bits // 2**16
    third = 3 - 6 * core

    def distance(s_at):
        h = rem(s_at, 8)
        own = div(h + 1, 2) * (2 * rem(h, 2) - 1)
        tail = jnp.where(h == 3, -third, jnp.where(h == 7, third, jnp.where(h == 6, 4, 18 - 4 * h)))
        return jnp.where((s_at >= 8) & (h >= 3), tail, own)

    def s_row(s_at):
        return rem(parity + div(s_at, 8), 2) * 8 + rem(y + distance(s_at) + 8, 8)

    def x_for_s(s_at):
        t = rem(s_row(s_at) + col - row + 32, 16)
        dx = rem(div(t, 4) - x + 4, 4)
        place = jnp.where(dx == 3, 2, jnp.where(dx == 2, 3, dx))
        far = rem(div(t, 2) + z_hi, 2)
        return far * 8 + place * 2 + rem(t + core, 2)

    def s_for_x(x_at):
        place = rem(div(x_at, 2), 4)
        dx = jnp.where(place == 3, 2, jnp.where(place == 2, 3, place))
        t = rem(x + dx, 4) * 4 + rem(z_hi + div(x_at, 8), 2) * 2 + rem(core + x_at, 2)
        u = rem(t + row - col + 16, 16)
        dy = rem(u - y + 8, 8)
        dy = jnp.where(dy > 4, dy - 8, dy)
        own = jnp.where(dy > 0, 2 * dy - 1, -2 * dy)
        tail = jnp.where(dy == third, 7, jnp.where(dy == -third, 3, jnp.where(dy == 4, 6, own + 1)))
        tail = jnp.where(own < 3, own, tail)
        return jnp.where(rem(div(u, 8) + parity, 2) == 1, 8 + tail, own)

    def multiply(s_at, x_at):
        names = x_tiles[x_at, DATA_X:, :]
        for wide in range(WIDE_X):
            stored, column = [], []
            for slot in range(SLOTS_X):
                index = wide * SLOTS_X + slot
                stored.append(x_tiles[x_at, index * BLOCK : (index + 1) * BLOCK, :])
                column.append(jnp.broadcast_to(names[index : index + 1, :], (BLOCK, LANES)))
            for j in range(COLS):
                placed = jnp.zeros((BLOCK, LANES), jnp.bfloat16)
                for slot in range(SLOTS_X):
                    placed = jnp.where(column[slot] == j, stored[slot], placed)
                x_dense[j * BLOCK : (j + 1) * BLOCK, wide * LANES : (wide + 1) * LANES] = placed
        names = s_tiles[s_at, DATA_S:, :]
        for wide in range(WIDE_S):
            stored, column = [], []
            for slot in range(SLOTS_S):
                index = wide * SLOTS_S + slot
                stored.append(s_tiles[s_at, index * BLOCK : (index + 1) * BLOCK, :])
                column.append(jnp.broadcast_to(names[index : index + 1, :], (BLOCK, LANES)))
            for j in range(COLS):
                placed = jnp.zeros((BLOCK, LANES), jnp.bfloat16)
                for slot in range(SLOTS_S):
                    placed = jnp.where(column[slot] == j, stored[slot], placed)
                s_dense[j * BLOCK : (j + 1) * BLOCK, wide * LANES : (wide + 1) * LANES] = placed
        total[...] += jnp.dot(s_dense[...], x_dense[...], preferred_element_type=jnp.float32)

        @pl.when(s_row(s_at) == 0)
        def _():
            total[...] -= 3.0 * x_dense[...].astype(jnp.float32)

    def happen(step, first, last):
        if last - first == 1:
            for entry in events.get(first, ()):
                entry()
        elif any(first <= turn < last for turn in events):
            middle = (first + last) // 2
            lax.cond(
                step < middle,
                lambda: happen(step, first, middle),
                lambda: happen(step, middle, last),
            )

    def body(step, arrived):
        s_count, x_count = arrived
        happen(step, 0, turns)
        by_x = (jnp.where(step < 16, low_bits, high_bits) >> rem(step, 16)) & 1
        s_at = jnp.where(by_x == 1, s_for_x(x_count), s_count)
        x_at = jnp.where(by_x == 1, x_count, x_for_s(s_count))
        ready = jnp.where(by_x == 1, s_at < s_count, x_at < x_count)

        @pl.when(ready)
        def _():
            multiply(s_at, x_at)

        return s_count + 1 - by_x, x_count + by_x

    lax.fori_loop(0, turns, body, (jnp.int32(0), jnp.int32(0)))
    out_ref[...] = (-0.5 * total[...]).astype(jnp.bfloat16)
    assert len(sends) == N_SENDS, len(sends)
    for index, ref in enumerate(sends):
        pltpu.make_async_remote_copy(
            src_ref=ref(), dst_ref=ref(), send_sem=sent.at[index], recv_sem=x_recv.at[0, 0],
            device_id=sibling, device_id_type=MESH,
        ).wait_send()


N_SENDS = 60


def shards(a_vals, a_cols, a_count, b_vals, b_cols, b_count):
    x_in = a_vals.reshape(ROWS, SLOTS_X, BLOCK, BLOCK).transpose(1, 0, 2, 3)
    x_in = x_in.reshape(SLOTS_X, ROWS * BLOCK, BLOCK)
    s_in = b_vals.reshape(COLS, SLOTS_S, BLOCK, BLOCK).transpose(1, 0, 2, 3)
    s_in = s_in.reshape(SLOTS_S, COLS * BLOCK, BLOCK)
    blocks = pl.BlockSpec(memory_space=pltpu.VMEM)
    turned = pl.pallas_call(
        kernel,
        out_shape=jax.ShapeDtypeStruct((COLS * BLOCK, ROWS * BLOCK), jnp.bfloat16),
        in_specs=[pl.BlockSpec(memory_space=pl.ANY)] * 4 + [blocks] * 2,
        out_specs=blocks,
        scratch_shapes=[
            pltpu.SMEM((ROWS, SLOTS_X), jnp.int32),
            pltpu.SMEM((ROWS,), jnp.int32),
            pltpu.SMEM((SLOTS_S, COLS), jnp.int32),
            pltpu.SMEM((COLS,), jnp.int32),
            pltpu.SemaphoreType.DMA((4,)),
            pltpu.VMEM((16, WIRE_X, LANES), jnp.bfloat16),
            pltpu.VMEM((16, WIRE_S, LANES), jnp.bfloat16),
            pltpu.VMEM((COLS * BLOCK, ROWS * BLOCK), jnp.bfloat16),
            pltpu.VMEM((COLS * BLOCK, COLS * BLOCK), jnp.bfloat16),
            pltpu.VMEM((COLS * BLOCK, ROWS * BLOCK), jnp.float32),
            pltpu.VMEM((META, LANES), jnp.float32),
            pltpu.SemaphoreType.DMA((16, 2)),
            pltpu.SemaphoreType.DMA((16, 2)),
            pltpu.SemaphoreType.DMA((N_SENDS,)),
        ],
        compiler_params=pltpu.CompilerParams(
            collective_id=0, has_side_effects=True, vmem_limit_bytes=40 * 1024 * 1024
        ),
        name="gather_multiply",
    )(a_cols[0, 0], a_count[0, 0], b_cols[0, 0].T, b_count[0, 0], x_in, s_in)
    return turned.T


def solution(mesh):
    in_specs = (
        P("row", "col", None, None, None),
        P("row", "col", None, None),
        P("row", "col", None),
        P("row", "col", None, None, None),
        P("row", "col", None, None),
        P("row", "col", None),
    )
    out_specs = P("row", "col")
    return jax.shard_map(shards, mesh=mesh, in_specs=in_specs, out_specs=out_specs, check_vma=False)
```

```python
import functools

import jax
import jax.numpy as jnp
from jax import lax
from jax.experimental import pallas as pl
from jax.experimental.pallas import tpu as pltpu
from jax.sharding import PartitionSpec as P

BLOCK = 96
LANES = 128
ROWS = 4
SLOTS_X = 5
COLS = 8
SLOTS_S = 2
WIDE_X = ROWS * BLOCK // LANES
WIDE_S = COLS * BLOCK // LANES
DATA_X = WIDE_X * SLOTS_X * BLOCK
DATA_S = WIDE_S * SLOTS_S * BLOCK
META = 16
WIRE_X = DATA_X + META
WIRE_S = DATA_S + META
SPLIT_X = (0, 720, WIRE_X)
SPLIT_S = (0, 576, WIRE_S)
MESH = pl.DeviceIdType.MESH
AROUND = (0, 1, 3, 2)
HALVES = (0, 1)
OWN = {0: 0, 1: 1, -1: 2, 2: 3, -2: 4, 3: 5, -3: 6, 4: 7}
OTHER = {0: 8, 1: 9, -1: 10, 2: 12, -2: 13, 4: 14}
BY_PAIR, BY_RING = 11, 15


def x_slot(other, dx, sibling=0):
    return 8 * other + 2 * AROUND.index(dx % 4) + sibling


def div(number, by):
    return lax.div(number, jnp.int32(by))


def rem(number, by):
    return lax.rem(number, jnp.int32(by))


def nt(left, right):
    return lax.dot_general(
        left, right, (((1,), (1,)), ((), ())), preferred_element_type=jnp.float32
    )


def kernel(
    a_cols_in, a_count_in, b_cols_in, b_count_in, x_in, s_in, out_ref,
    a_cols, a_count, b_cols, b_count, scalars_came, x_tiles, s_tiles, x_dense, s_dense, total, meta, x_recv, s_recv, sent,
):
    row, col = lax.axis_index("row"), lax.axis_index("col")
    y, z_lo = rem(row, 8), div(row, 8)
    core, z_hi, x = rem(col, 2), rem(div(col, 2), 2), div(col, 4)
    parity = rem(z_lo, 2)

    def at(x_at, y_at, z_lo_at, z_hi_at, core_at):
        return (z_lo_at * 8 + y_at, (x_at * 2 + z_hi_at) * 2 + core_at)

    def along_x(d):
        return at(rem(x + d + 4, 4), y, z_lo, z_hi, core)

    def along_y(d):
        return at(x, rem(y + d + 8, 8), z_lo, z_hi, core)

    pair_chip = at(x, y, z_lo + 1 - 2 * parity, z_hi, core)
    far_chip = at(x, y, z_lo, 1 - z_hi, core)
    sibling = at(x, y, z_lo, z_hi, 1 - core)
    near_chips = (along_x(1), along_x(-1), along_y(1), along_y(-1), pair_chip, sibling)
    barrier = pltpu.get_barrier_semaphore()

    def greet(device):
        pl.semaphore_signal(barrier, inc=1, device_id=device, device_id_type=MESH)

    for device in near_chips:
        greet(device)
    scalars = [
        pltpu.make_async_copy(source, target, scalars_came.at[index])
        for index, (source, target) in enumerate(
            ((a_cols_in, a_cols), (a_count_in, a_count), (b_cols_in, b_cols), (b_count_in, b_count))
        )
    ]
    for copy in scalars:
        copy.start()

    sends = []

    def s_part(slot, half):
        start = SPLIT_S[half]
        return s_tiles.at[slot, pl.ds(start, SPLIT_S[half + 1] - start)]

    def x_part(slot, half):
        start = SPLIT_X[half]
        return x_tiles.at[slot, pl.ds(start, SPLIT_X[half + 1] - start)]

    def send(part, arrived, source, target, device, half, index=None):
        if index is None:
            index = len(sends)
            sends.append(functools.partial(part, source, half))
        pltpu.make_async_remote_copy(
            src_ref=part(source, half), dst_ref=part(target, half),
            send_sem=sent.at[index], recv_sem=arrived.at[target, half],
            device_id=device, device_id_type=MESH,
        ).start()

    def wait(part, arrived, slot, half):
        ref = part(slot, half)
        pltpu.make_async_remote_copy(
            src_ref=ref, dst_ref=ref, send_sem=sent.at[0], recv_sem=arrived.at[slot, half],
            device_id=sibling, device_id_type=MESH,
        ).wait_recv()

    s_copy = functools.partial(send, s_part, s_recv)
    x_copy = functools.partial(send, x_part, x_recv)
    s_wait = functools.partial(wait, s_part, s_recv)
    x_wait = functools.partial(wait, x_part, x_recv)

    lane = lax.broadcasted_iota(jnp.int32, (1, LANES), 1)
    unit = (
        lax.broadcasted_iota(jnp.int32, (BLOCK, BLOCK), 0)
        == lax.broadcasted_iota(jnp.int32, (BLOCK, BLOCK), 1)
    ).astype(jnp.bfloat16)

    def lane_columns(where, number, wide, slot):
        first = wide * LANES // BLOCK
        values = []
        for block in (first, first + 1):
            live = slot < number[block]
            values.append(jnp.where(live, where(block, slot), -1).astype(jnp.float32))
        return jnp.where(lane + wide * LANES < (first + 1) * BLOCK, values[0], values[1])

    for copy in scalars:
        copy.wait()
    meta[...] = jnp.full_like(meta, -1.0)
    for wide in range(WIDE_S):
        for slot in range(SLOTS_S):
            index = wide * SLOTS_S + slot
            meta[index : index + 1, :] = lane_columns(lambda block, slot: b_cols[slot, block], b_count, wide, slot)
    s_tiles[0, DATA_S:, :] = meta[...].astype(jnp.bfloat16)
    for slot in range(SLOTS_S):
        turned = nt(unit, s_in[slot]).astype(jnp.bfloat16)
        for wide in range(WIDE_S):
            index = wide * SLOTS_S + slot
            s_tiles[0, index * BLOCK : (index + 1) * BLOCK, :] = turned[
                :, wide * LANES : (wide + 1) * LANES
            ]
    pl.semaphore_wait(barrier, len(near_chips) + z_hi)
    greet(far_chip)
    for half in HALVES:
        s_copy(0, OWN[-1], along_y(1), half)
        s_copy(0, OWN[1], along_y(-1), half)

    meta[...] = jnp.full_like(meta, -1.0)
    for wide in range(WIDE_X):
        for slot in range(SLOTS_X):
            index = wide * SLOTS_X + slot
            meta[index : index + 1, :] = lane_columns(lambda block, slot: a_cols[block, slot], a_count, wide, slot)
    x_tiles[0, DATA_X:, :] = meta[...].astype(jnp.bfloat16)
    for slot in range(SLOTS_X):
        turned = nt(unit, x_in[slot]).astype(jnp.bfloat16)
        for wide in range(WIDE_X):
            index = wide * SLOTS_X + slot
            x_tiles[0, index * BLOCK : (index + 1) * BLOCK, :] = turned[
                :, wide * LANES : (wide + 1) * LANES
            ]
    far_sends = len(sends)
    sends.extend(functools.partial(x_part, 0, half) for half in HALVES)

    def x_leave():
        for half in HALVES:
            x_copy(0, x_slot(1, 0), far_chip, half, far_sends + half)

    def x_leave_late():
        @pl.when(z_hi == 0)
        def _():
            pl.semaphore_wait(barrier, 1)
            x_leave()

    pl.when(z_hi == 1)(x_leave)
    for half in HALVES:
        x_copy(0, x_slot(0, -1), along_x(1), half)
        x_copy(0, x_slot(0, 1), along_x(-1), half)
    for half in HALVES:
        x_copy(0, x_slot(0, 0, 1), sibling, half)
    for half in HALVES:
        s_copy(0, OTHER[0], pair_chip, half)
    total[...] = jnp.zeros_like(total)

    def s_ring(slots, near, half):
        for sign in (1, -1):
            here = slots[sign * near]
            s_wait(here, half)
            s_copy(here, slots[sign * (near + 1)], along_y(-sign), half)

    def x_near(other, half):
        for d in (1, -1):
            here = x_slot(other, d)
            x_wait(here, half)
            if (half == 0) == (d == 1):
                x_copy(here, x_slot(other, 2), along_x(-d), half)
            x_copy(here, here + 1, sibling, half)

    def x_across(other):
        here = x_slot(other, 2)
        for half in HALVES:
            x_wait(here, half)
            x_copy(here, here + 1, sibling, half)

    def x_far(half):
        here = x_slot(1, 0)
        x_wait(here, half)
        x_copy(here, x_slot(1, -1), along_x(1), half)
        x_copy(here, x_slot(1, 1), along_x(-1), half)
        x_copy(here, here + 1, sibling, half)

    def x_sibling(other, dx):
        for half in HALVES:
            x_wait(x_slot(other, dx, 1), half)

    pair_third = OWN[-3] - core
    ring_second, other_second = OTHER[2] + core, OTHER[-2] - core
    ring_chip = along_y(2 * core - 1)

    def s_third_first():
        s_wait(OWN[3], 0)
        s_copy(OWN[3], OWN[4], along_y(-1), 0)
        s_wait(OWN[-3], 0)
        s_copy(pair_third, BY_PAIR, pair_chip, 0)

    def s_third_last():
        s_wait(OWN[-3], 1)
        s_copy(OWN[-3], OWN[4], along_y(1), 1)
        s_wait(OWN[3], 1)
        s_copy(pair_third, BY_PAIR, pair_chip, 1)

    def s_other_start():
        for half in HALVES:
            s_wait(OTHER[0], half)
            s_copy(OTHER[0], OTHER[1], along_y(-1), half)
            s_copy(OTHER[0], OTHER[-1], along_y(1), half)

    def s_fourth():
        for half in HALVES:
            s_wait(OWN[4], half)
            s_copy(OWN[4], OTHER[4], pair_chip, half)

    def s_other_second(half):
        s_wait(ring_second, half)
        s_copy(ring_second, BY_RING, ring_chip, half)

    def s_last(slot):
        for half in HALVES:
            s_wait(slot, half)

    left = [0]

    def sends_leave(end):
        for index in range(left[0], end):
            ref = sends[index]()
            pltpu.make_async_remote_copy(
                src_ref=ref, dst_ref=ref, send_sem=sent.at[index], recv_sem=x_recv.at[0, 0],
                device_id=sibling, device_id_type=MESH,
            ).wait_send()
        left[0] = end

    part = functools.partial
    plan = (
        "S", "X",
        part(s_ring, OWN, 1, 0), x_leave_late, part(x_sibling, 0, 0), "X",
        part(s_ring, OWN, 1, 1), "S", "S",
        part(s_ring, OWN, 2, 0), part(x_near, 0, 0), part(x_near, 0, 1), "X",
        part(s_ring, OWN, 2, 1), "S", "S",
        part(x_sibling, 0, 1), "X", "X",
        s_third_first, part(x_sibling, 0, -1), "X", part(x_across, 0), s_third_last, part(x_far, 0), "S", "S",
        s_other_start, "X", part(x_sibling, 0, 2), "X",
        s_fourth, part(x_far, 1), part(sends_leave, 20), "S", "S",
        "X", part(s_ring, OTHER, 1, 0), part(x_near, 1, 0), part(x_sibling, 1, 0), "X",
        part(s_ring, OTHER, 1, 1), part(x_near, 1, 1), "S", "S", "X",
        part(s_other_second, 0), part(x_sibling, 1, 1), "X", "X", part(s_last, BY_PAIR), "S",
        part(x_sibling, 1, -1), "X", part(x_across, 1), "X",
        part(s_other_second, 1), part(sends_leave, 40),
        part(s_last, other_second), "S", "S",
        part(x_sibling, 1, 2), "X",
        part(s_last, OTHER[4]), "S",
        part(s_last, BY_RING), "S",
    )
    events, turns, bits = {}, 0, 0
    for entry in plan:
        if entry in ("S", "X"):
            bits += (entry == "X") << turns
            turns += 1
        else:
            events.setdefault(turns, []).append(entry)
    low_bits, high_bits = bits % 2**16, bits // 2**16
    third = 3 - 6 * core

    def distance(s_at):
        h = rem(s_at, 8)
        own = div(h + 1, 2) * (2 * rem(h, 2) - 1)
        tail = jnp.where(h == 3, -third, jnp.where(h == 7, third, jnp.where(h == 6, 4, 18 - 4 * h)))
        return jnp.where((s_at >= 8) & (h >= 3), tail, own)

    def s_row(s_at):
        return rem(parity + div(s_at, 8), 2) * 8 + rem(y + distance(s_at) + 8, 8)

    def x_for_s(s_at):
        t = rem(s_row(s_at) + col - row + 32, 16)
        dx = rem(div(t, 4) - x + 4, 4)
        place = jnp.where(dx == 3, 2, jnp.where(dx == 2, 3, dx))
        far = rem(div(t, 2) + z_hi, 2)
        return far * 8 + place * 2 + rem(t + core, 2)

    def s_for_x(x_at):
        place = rem(div(x_at, 2), 4)
        dx = jnp.where(place == 3, 2, jnp.where(place == 2, 3, place))
        t = rem(x + dx, 4) * 4 + rem(z_hi + div(x_at, 8), 2) * 2 + rem(core + x_at, 2)
        u = rem(t + row - col + 16, 16)
        dy = rem(u - y + 8, 8)
        dy = jnp.where(dy > 4, dy - 8, dy)
        own = jnp.where(dy > 0, 2 * dy - 1, -2 * dy)
        tail = jnp.where(dy == third, 7, jnp.where(dy == -third, 3, jnp.where(dy == 4, 6, own + 1)))
        tail = jnp.where(own < 3, own, tail)
        return jnp.where(rem(div(u, 8) + parity, 2) == 1, 8 + tail, own)

    def multiply(s_at, x_at):
        names = x_tiles[x_at, DATA_X:, :]
        for wide in range(WIDE_X):
            stored, column = [], []
            for slot in range(SLOTS_X):
                index = wide * SLOTS_X + slot
                stored.append(x_tiles[x_at, index * BLOCK : (index + 1) * BLOCK, :])
                column.append(jnp.broadcast_to(names[index : index + 1, :], (BLOCK, LANES)))
            for j in range(COLS):
                placed = jnp.zeros((BLOCK, LANES), jnp.bfloat16)
                for slot in range(SLOTS_X):
                    placed = jnp.where(column[slot] == j, stored[slot], placed)
                x_dense[j * BLOCK : (j + 1) * BLOCK, wide * LANES : (wide + 1) * LANES] = placed
        names = s_tiles[s_at, DATA_S:, :]
        for wide in range(WIDE_S):
            stored, column = [], []
            for slot in range(SLOTS_S):
                index = wide * SLOTS_S + slot
                stored.append(s_tiles[s_at, index * BLOCK : (index + 1) * BLOCK, :])
                column.append(jnp.broadcast_to(names[index : index + 1, :], (BLOCK, LANES)))
            for j in range(COLS):
                placed = jnp.zeros((BLOCK, LANES), jnp.bfloat16)
                for slot in range(SLOTS_S):
                    placed = jnp.where(column[slot] == j, stored[slot], placed)
                s_dense[j * BLOCK : (j + 1) * BLOCK, wide * LANES : (wide + 1) * LANES] = placed
        total[...] += jnp.dot(s_dense[...], x_dense[...], preferred_element_type=jnp.float32)

        @pl.when(s_row(s_at) == 0)
        def _():
            total[...] -= 3.0 * x_dense[...].astype(jnp.float32)

    def happen(step, first, last):
        if last - first == 1:
            for entry in events.get(first, ()):
                entry()
        elif any(first <= turn < last for turn in events):
            middle = (first + last) // 2
            lax.cond(
                step < middle,
                lambda: happen(step, first, middle),
                lambda: happen(step, middle, last),
            )

    def body(step, arrived):
        s_count, x_count = arrived
        happen(step, 0, turns)
        by_x = (jnp.where(step < 16, low_bits, high_bits) >> rem(step, 16)) & 1
        s_at = jnp.where(by_x == 1, s_for_x(x_count), s_count)
        x_at = jnp.where(by_x == 1, x_count, x_for_s(s_count))
        ready = jnp.where(by_x == 1, s_at < s_count, x_at < x_count)

        @pl.when(ready)
        def _():
            multiply(s_at, x_at)

        return s_count + 1 - by_x, x_count + by_x

    lax.fori_loop(0, turns, body, (jnp.int32(0), jnp.int32(0)))
    out_ref[...] = (-0.5 * total[...]).astype(jnp.bfloat16)
    assert len(sends) == N_SENDS, len(sends)
    sends_leave(len(sends))


N_SENDS = 60


def shards(a_vals, a_cols, a_count, b_vals, b_cols, b_count):
    x_in = a_vals.reshape(ROWS, SLOTS_X, BLOCK, BLOCK).transpose(1, 0, 2, 3)
    x_in = x_in.reshape(SLOTS_X, ROWS * BLOCK, BLOCK)
    b_vals, x_in = lax.optimization_barrier((b_vals, x_in))
    s_in = b_vals.reshape(COLS, SLOTS_S, BLOCK, BLOCK).transpose(1, 0, 2, 3)
    s_in = s_in.reshape(SLOTS_S, COLS * BLOCK, BLOCK)
    blocks = pl.BlockSpec(memory_space=pltpu.VMEM)
    turned = pl.pallas_call(
        kernel,
        out_shape=jax.ShapeDtypeStruct((COLS * BLOCK, ROWS * BLOCK), jnp.bfloat16),
        in_specs=[pl.BlockSpec(memory_space=pl.ANY)] * 4 + [blocks] * 2,
        out_specs=blocks,
        scratch_shapes=[
            pltpu.SMEM((ROWS, SLOTS_X), jnp.int32),
            pltpu.SMEM((ROWS,), jnp.int32),
            pltpu.SMEM((SLOTS_S, COLS), jnp.int32),
            pltpu.SMEM((COLS,), jnp.int32),
            pltpu.SemaphoreType.DMA((4,)),
            pltpu.VMEM((16, WIRE_X, LANES), jnp.bfloat16),
            pltpu.VMEM((16, WIRE_S, LANES), jnp.bfloat16),
            pltpu.VMEM((COLS * BLOCK, ROWS * BLOCK), jnp.bfloat16),
            pltpu.VMEM((COLS * BLOCK, COLS * BLOCK), jnp.bfloat16),
            pltpu.VMEM((COLS * BLOCK, ROWS * BLOCK), jnp.float32),
            pltpu.VMEM((META, LANES), jnp.float32),
            pltpu.SemaphoreType.DMA((16, 2)),
            pltpu.SemaphoreType.DMA((16, 2)),
            pltpu.SemaphoreType.DMA((N_SENDS,)),
        ],
        compiler_params=pltpu.CompilerParams(
            collective_id=0, has_side_effects=True, vmem_limit_bytes=40 * 1024 * 1024
        ),
        name="gather_multiply",
    )(
        *(
            pltpu.with_memory_space_constraint(number, pltpu.HBM)
            for number in (a_cols[0, 0], a_count[0, 0], b_cols[0, 0].T, b_count[0, 0])
        ),
        x_in,
        s_in,
    )
    return turned.T


def solution(mesh):
    in_specs = (
        P("row", "col", None, None, None),
        P("row", "col", None, None),
        P("row", "col", None),
        P("row", "col", None, None, None),
        P("row", "col", None, None),
        P("row", "col", None),
    )
    out_specs = P("row", "col")
    return jax.shard_map(shards, mesh=mesh, in_specs=in_specs, out_specs=out_specs, check_vma=False)
```

```python
import functools

import jax
import jax.numpy as jnp
from jax import lax
from jax.experimental import pallas as pl
from jax.experimental.pallas import tpu as pltpu
from jax.sharding import PartitionSpec as P

BLOCK = 96
LANES = 128
ROWS = 4
SLOTS_X = 5
COLS = 8
SLOTS_S = 2
WIDE_X = ROWS * BLOCK // LANES
WIDE_S = COLS * BLOCK // LANES
DATA_X = WIDE_X * SLOTS_X * BLOCK
DATA_S = WIDE_S * SLOTS_S * BLOCK
META = 16
WIRE_X = DATA_X + META
WIRE_S = DATA_S + META
SPLIT_X = (0, 720, WIRE_X)
SPLIT_S = (0, 576, WIRE_S)
MESH = pl.DeviceIdType.MESH
AROUND = (0, 1, 3, 2)
HALVES = (0, 1)
OWN = {0: 0, 1: 1, -1: 2, 2: 3, -2: 4, 3: 5, -3: 6, 4: 7}
OTHER = {0: 8, 1: 9, -1: 10, 2: 12, -2: 13, 4: 14}
BY_PAIR, BY_RING = 11, 15


def x_slot(other, dx, sibling=0):
    return 8 * other + 2 * AROUND.index(dx % 4) + sibling


def div(number, by):
    return lax.div(number, jnp.int32(by))


def rem(number, by):
    return lax.rem(number, jnp.int32(by))


def nt(left, right):
    return lax.dot_general(
        left, right, (((1,), (1,)), ((), ())), preferred_element_type=jnp.float32
    )


def kernel(
    a_cols_in, a_count_in, b_cols_in, b_count_in, x_in, s_in, out_ref,
    a_cols, a_count, b_cols, b_count, scalars_came, x_tiles, s_tiles, x_dense, s_dense, total, meta, x_recv, s_recv, sent,
):
    row, col = lax.axis_index("row"), lax.axis_index("col")
    y, z_lo = rem(row, 8), div(row, 8)
    core, z_hi, x = rem(col, 2), rem(div(col, 2), 2), div(col, 4)
    parity = rem(z_lo, 2)

    def at(x_at, y_at, z_lo_at, z_hi_at, core_at):
        return (z_lo_at * 8 + y_at, (x_at * 2 + z_hi_at) * 2 + core_at)

    def along_x(d):
        return at(rem(x + d + 4, 4), y, z_lo, z_hi, core)

    def along_y(d):
        return at(x, rem(y + d + 8, 8), z_lo, z_hi, core)

    pair_chip = at(x, y, z_lo + 1 - 2 * parity, z_hi, core)
    far_chip = at(x, y, z_lo, 1 - z_hi, core)
    sibling = at(x, y, z_lo, z_hi, 1 - core)
    near_chips = (along_x(1), along_x(-1), along_y(1), along_y(-1), pair_chip, sibling)
    barrier = pltpu.get_barrier_semaphore()

    def greet(device):
        pl.semaphore_signal(barrier, inc=1, device_id=device, device_id_type=MESH)

    for device in near_chips:
        greet(device)
    scalars = [
        pltpu.make_async_copy(source, target, scalars_came.at[index])
        for index, (source, target) in enumerate(
            ((a_cols_in, a_cols), (a_count_in, a_count), (b_cols_in, b_cols), (b_count_in, b_count))
        )
    ]
    for copy in scalars:
        copy.start()

    sends = []

    def s_part(slot, half):
        start = SPLIT_S[half]
        return s_tiles.at[slot, pl.ds(start, SPLIT_S[half + 1] - start)]

    def x_part(slot, half):
        start = SPLIT_X[half]
        return x_tiles.at[slot, pl.ds(start, SPLIT_X[half + 1] - start)]

    def send(part, arrived, source, target, device, half, index=None):
        if index is None:
            index = len(sends)
            sends.append(functools.partial(part, source, half))
        pltpu.make_async_remote_copy(
            src_ref=part(source, half), dst_ref=part(target, half),
            send_sem=sent.at[index], recv_sem=arrived.at[target, half],
            device_id=device, device_id_type=MESH,
        ).start()

    def wait(part, arrived, slot, half):
        ref = part(slot, half)
        pltpu.make_async_remote_copy(
            src_ref=ref, dst_ref=ref, send_sem=sent.at[0], recv_sem=arrived.at[slot, half],
            device_id=sibling, device_id_type=MESH,
        ).wait_recv()

    s_copy = functools.partial(send, s_part, s_recv)
    x_copy = functools.partial(send, x_part, x_recv)
    s_wait = functools.partial(wait, s_part, s_recv)
    x_wait = functools.partial(wait, x_part, x_recv)

    lane = lax.broadcasted_iota(jnp.int32, (1, LANES), 1)
    unit = (
        lax.broadcasted_iota(jnp.int32, (BLOCK, BLOCK), 0)
        == lax.broadcasted_iota(jnp.int32, (BLOCK, BLOCK), 1)
    ).astype(jnp.bfloat16)

    def lane_columns(where, number, wide, slot):
        first = wide * LANES // BLOCK
        values = []
        for block in (first, first + 1):
            live = slot < number[block]
            values.append(jnp.where(live, where(block, slot), -1).astype(jnp.float32))
        return jnp.where(lane + wide * LANES < (first + 1) * BLOCK, values[0], values[1])

    for slot in range(SLOTS_S):
        turned = nt(unit, s_in[slot]).astype(jnp.bfloat16)
        for wide in range(WIDE_S):
            index = wide * SLOTS_S + slot
            s_tiles[0, index * BLOCK : (index + 1) * BLOCK, :] = turned[
                :, wide * LANES : (wide + 1) * LANES
            ]
    pl.semaphore_wait(barrier, len(near_chips) + z_hi)
    greet(far_chip)

    def s_start(half):
        s_copy(0, OWN[-1], along_y(1), half)
        s_copy(0, OWN[1], along_y(-1), half)

    s_start(0)
    for copy in scalars:
        copy.wait()
    meta[...] = jnp.full_like(meta, -1.0)
    for wide in range(WIDE_S):
        for slot in range(SLOTS_S):
            index = wide * SLOTS_S + slot
            meta[index : index + 1, :] = lane_columns(
                lambda block, slot: b_cols[slot, block], b_count, wide, slot
            )
    s_tiles[0, DATA_S:, :] = meta[...].astype(jnp.bfloat16)
    s_start(1)

    for slot in range(SLOTS_X):
        turned = nt(unit, x_in[slot]).astype(jnp.bfloat16)
        for wide in range(WIDE_X):
            index = wide * SLOTS_X + slot
            x_tiles[0, index * BLOCK : (index + 1) * BLOCK, :] = turned[
                :, wide * LANES : (wide + 1) * LANES
            ]

    def x_leave(half):
        x_copy(0, x_slot(1, 0), far_chip, half, N_SENDS - 2 + half)

    def x_leave_late():
        @pl.when(z_hi == 0)
        def _():
            pl.semaphore_wait(barrier, 1)
            for half in HALVES:
                x_leave(half)

    def x_start(half):
        pl.when(z_hi == 1)(functools.partial(x_leave, half))
        x_copy(0, x_slot(0, -1), along_x(1), half)
        x_copy(0, x_slot(0, 1), along_x(-1), half)

    x_start(0)
    meta[...] = jnp.full_like(meta, -1.0)
    for wide in range(WIDE_X):
        for slot in range(SLOTS_X):
            index = wide * SLOTS_X + slot
            meta[index : index + 1, :] = lane_columns(
                lambda block, slot: a_cols[block, slot], a_count, wide, slot
            )
    x_tiles[0, DATA_X:, :] = meta[...].astype(jnp.bfloat16)
    x_start(1)
    for half in HALVES:
        x_copy(0, x_slot(0, 0, 1), sibling, half)
    for half in HALVES:
        s_copy(0, OTHER[0], pair_chip, half)
    total[...] = jnp.zeros_like(total)

    def s_ring(slots, near, half):
        for sign in (1, -1):
            here = slots[sign * near]
            s_wait(here, half)
            s_copy(here, slots[sign * (near + 1)], along_y(-sign), half)

    def x_near(other, half):
        for d in (1, -1):
            here = x_slot(other, d)
            x_wait(here, half)
            if (half == 0) == (d == 1):
                x_copy(here, x_slot(other, 2), along_x(-d), half)
            x_copy(here, here + 1, sibling, half)

    def x_across(other):
        here = x_slot(other, 2)
        for half in HALVES:
            x_wait(here, half)
            x_copy(here, here + 1, sibling, half)

    def x_far(half):
        here = x_slot(1, 0)
        x_wait(here, half)
        x_copy(here, x_slot(1, -1), along_x(1), half)
        x_copy(here, x_slot(1, 1), along_x(-1), half)
        x_copy(here, here + 1, sibling, half)

    def x_sibling(other, dx):
        for half in HALVES:
            x_wait(x_slot(other, dx, 1), half)

    pair_third = OWN[-3] - core
    ring_second, other_second = OTHER[2] + core, OTHER[-2] - core
    ring_chip = along_y(2 * core - 1)

    def s_third_first():
        s_wait(OWN[3], 0)
        s_copy(OWN[3], OWN[4], along_y(-1), 0)
        s_wait(OWN[-3], 0)
        s_copy(pair_third, BY_PAIR, pair_chip, 0)

    def s_third_last():
        s_wait(OWN[-3], 1)
        s_copy(OWN[-3], OWN[4], along_y(1), 1)
        s_wait(OWN[3], 1)
        s_copy(pair_third, BY_PAIR, pair_chip, 1)

    def s_other_start():
        for half in HALVES:
            s_wait(OTHER[0], half)
            s_copy(OTHER[0], OTHER[1], along_y(-1), half)
            s_copy(OTHER[0], OTHER[-1], along_y(1), half)

    def s_fourth():
        for half in HALVES:
            s_wait(OWN[4], half)
            s_copy(OWN[4], OTHER[4], pair_chip, half)

    def s_other_second(half):
        s_wait(ring_second, half)
        s_copy(ring_second, BY_RING, ring_chip, half)

    def s_last(slot):
        for half in HALVES:
            s_wait(slot, half)

    left = [0]

    def sends_leave(end):
        for index in range(left[0], end):
            ref = sends[index]()
            pltpu.make_async_remote_copy(
                src_ref=ref, dst_ref=ref, send_sem=sent.at[index], recv_sem=x_recv.at[0, 0],
                device_id=sibling, device_id_type=MESH,
            ).wait_send()
        left[0] = end

    part = functools.partial
    plan = (
        "S", "X",
        part(s_ring, OWN, 1, 0), x_leave_late, part(x_sibling, 0, 0), "X",
        part(s_ring, OWN, 1, 1), "S", "S",
        part(s_ring, OWN, 2, 0), part(x_near, 0, 0), part(x_near, 0, 1), "X",
        part(s_ring, OWN, 2, 1), "S", "S",
        part(x_sibling, 0, 1), "X", "X",
        s_third_first, part(x_sibling, 0, -1), "X", part(x_across, 0), s_third_last, part(x_far, 0), "S", "S",
        s_other_start, "X", part(x_sibling, 0, 2), "X",
        s_fourth, part(x_far, 1), part(sends_leave, 20), "S", "S",
        "X", part(s_ring, OTHER, 1, 0), part(x_near, 1, 0), part(x_sibling, 1, 0), "X",
        part(s_ring, OTHER, 1, 1), part(x_near, 1, 1), "S", "S", "X",
        part(s_other_second, 0), part(x_sibling, 1, 1), "X", "X", part(s_last, BY_PAIR), "S",
        part(x_sibling, 1, -1), "X", part(x_across, 1), "X",
        part(s_other_second, 1), part(sends_leave, 40),
        part(s_last, other_second), "S", "S",
        part(x_sibling, 1, 2), "X",
        part(s_last, OTHER[4]), "S",
        part(s_last, BY_RING), "S",
    )
    events, turns, bits = {}, 0, 0
    for entry in plan:
        if entry in ("S", "X"):
            bits += (entry == "X") << turns
            turns += 1
        else:
            events.setdefault(turns, []).append(entry)
    low_bits, high_bits = bits % 2**16, bits // 2**16
    third = 3 - 6 * core

    def distance(s_at):
        h = rem(s_at, 8)
        own = div(h + 1, 2) * (2 * rem(h, 2) - 1)
        tail = jnp.where(h == 3, -third, jnp.where(h == 7, third, jnp.where(h == 6, 4, 18 - 4 * h)))
        return jnp.where((s_at >= 8) & (h >= 3), tail, own)

    def s_row(s_at):
        return rem(parity + div(s_at, 8), 2) * 8 + rem(y + distance(s_at) + 8, 8)

    def x_for_s(s_at):
        t = rem(s_row(s_at) + col - row + 32, 16)
        dx = rem(div(t, 4) - x + 4, 4)
        place = jnp.where(dx == 3, 2, jnp.where(dx == 2, 3, dx))
        far = rem(div(t, 2) + z_hi, 2)
        return far * 8 + place * 2 + rem(t + core, 2)

    def s_for_x(x_at):
        place = rem(div(x_at, 2), 4)
        dx = jnp.where(place == 3, 2, jnp.where(place == 2, 3, place))
        t = rem(x + dx, 4) * 4 + rem(z_hi + div(x_at, 8), 2) * 2 + rem(core + x_at, 2)
        u = rem(t + row - col + 16, 16)
        dy = rem(u - y + 8, 8)
        dy = jnp.where(dy > 4, dy - 8, dy)
        own = jnp.where(dy > 0, 2 * dy - 1, -2 * dy)
        tail = jnp.where(dy == third, 7, jnp.where(dy == -third, 3, jnp.where(dy == 4, 6, own + 1)))
        tail = jnp.where(own < 3, own, tail)
        return jnp.where(rem(div(u, 8) + parity, 2) == 1, 8 + tail, own)

    def multiply(s_at, x_at):
        names = x_tiles[x_at, DATA_X:, :]
        for wide in range(WIDE_X):
            stored, column = [], []
            for slot in range(SLOTS_X):
                index = wide * SLOTS_X + slot
                stored.append(x_tiles[x_at, index * BLOCK : (index + 1) * BLOCK, :])
                column.append(jnp.broadcast_to(names[index : index + 1, :], (BLOCK, LANES)))
            for j in range(COLS):
                placed = jnp.zeros((BLOCK, LANES), jnp.bfloat16)
                for slot in range(SLOTS_X):
                    placed = jnp.where(column[slot] == j, stored[slot], placed)
                x_dense[j * BLOCK : (j + 1) * BLOCK, wide * LANES : (wide + 1) * LANES] = placed
        names = s_tiles[s_at, DATA_S:, :]
        for wide in range(WIDE_S):
            stored, column = [], []
            for slot in range(SLOTS_S):
                index = wide * SLOTS_S + slot
                stored.append(s_tiles[s_at, index * BLOCK : (index + 1) * BLOCK, :])
                column.append(jnp.broadcast_to(names[index : index + 1, :], (BLOCK, LANES)))
            for j in range(COLS):
                placed = jnp.zeros((BLOCK, LANES), jnp.bfloat16)
                for slot in range(SLOTS_S):
                    placed = jnp.where(column[slot] == j, stored[slot], placed)
                s_dense[j * BLOCK : (j + 1) * BLOCK, wide * LANES : (wide + 1) * LANES] = placed
        total[...] += jnp.dot(s_dense[...], x_dense[...], preferred_element_type=jnp.float32)

        @pl.when(s_row(s_at) == 0)
        def _():
            total[...] -= 3.0 * x_dense[...].astype(jnp.float32)

    def happen(step, first, last):
        if last - first == 1:
            for entry in events.get(first, ()):
                entry()
        elif any(first <= turn < last for turn in events):
            middle = (first + last) // 2
            lax.cond(
                step < middle,
                lambda: happen(step, first, middle),
                lambda: happen(step, middle, last),
            )

    def body(step, arrived):
        s_count, x_count = arrived
        happen(step, 0, turns)
        by_x = (jnp.where(step < 16, low_bits, high_bits) >> rem(step, 16)) & 1
        s_at = jnp.where(by_x == 1, s_for_x(x_count), s_count)
        x_at = jnp.where(by_x == 1, x_count, x_for_s(s_count))
        ready = jnp.where(by_x == 1, s_at < s_count, x_at < x_count)

        @pl.when(ready)
        def _():
            multiply(s_at, x_at)

        return s_count + 1 - by_x, x_count + by_x

    lax.fori_loop(0, turns, body, (jnp.int32(0), jnp.int32(0)))
    out_ref[...] = (-0.5 * total[...]).astype(jnp.bfloat16)
    sends.extend(functools.partial(x_part, 0, half) for half in HALVES)
    assert len(sends) == N_SENDS, len(sends)
    sends_leave(N_SENDS)


N_SENDS = 60


def shards(a_vals, a_cols, a_count, b_vals, b_cols, b_count):
    x_in = a_vals.reshape(ROWS, SLOTS_X, BLOCK, BLOCK).transpose(1, 0, 2, 3)
    x_in = x_in.reshape(SLOTS_X, ROWS * BLOCK, BLOCK)
    b_vals, x_in = lax.optimization_barrier((b_vals, x_in))
    s_in = b_vals.reshape(COLS, SLOTS_S, BLOCK, BLOCK).transpose(1, 0, 2, 3)
    s_in = s_in.reshape(SLOTS_S, COLS * BLOCK, BLOCK)
    blocks = pl.BlockSpec(memory_space=pltpu.VMEM)
    turned = pl.pallas_call(
        kernel,
        out_shape=jax.ShapeDtypeStruct((COLS * BLOCK, ROWS * BLOCK), jnp.bfloat16),
        in_specs=[pl.BlockSpec(memory_space=pl.ANY)] * 4 + [blocks] * 2,
        out_specs=blocks,
        scratch_shapes=[
            pltpu.SMEM((ROWS, SLOTS_X), jnp.int32),
            pltpu.SMEM((ROWS,), jnp.int32),
            pltpu.SMEM((SLOTS_S, COLS), jnp.int32),
            pltpu.SMEM((COLS,), jnp.int32),
            pltpu.SemaphoreType.DMA((4,)),
            pltpu.VMEM((16, WIRE_X, LANES), jnp.bfloat16),
            pltpu.VMEM((16, WIRE_S, LANES), jnp.bfloat16),
            pltpu.VMEM((COLS * BLOCK, ROWS * BLOCK), jnp.bfloat16),
            pltpu.VMEM((COLS * BLOCK, COLS * BLOCK), jnp.bfloat16),
            pltpu.VMEM((COLS * BLOCK, ROWS * BLOCK), jnp.float32),
            pltpu.VMEM((META, LANES), jnp.float32),
            pltpu.SemaphoreType.DMA((16, 2)),
            pltpu.SemaphoreType.DMA((16, 2)),
            pltpu.SemaphoreType.DMA((N_SENDS,)),
        ],
        compiler_params=pltpu.CompilerParams(
            collective_id=0, has_side_effects=True, vmem_limit_bytes=40 * 1024 * 1024
        ),
        name="gather_multiply",
    )(
        *(
            pltpu.with_memory_space_constraint(number, pltpu.HBM)
            for number in (a_cols[0, 0], a_count[0, 0], b_cols[0, 0].T, b_count[0, 0])
        ),
        x_in,
        s_in,
    )
    return turned.T


def solution(mesh):
    in_specs = (
        P("row", "col", None, None, None),
        P("row", "col", None, None),
        P("row", "col", None),
        P("row", "col", None, None, None),
        P("row", "col", None, None),
        P("row", "col", None),
    )
    out_specs = P("row", "col")
    return jax.shard_map(shards, mesh=mesh, in_specs=in_specs, out_specs=out_specs, check_vma=False)
```

```python
import functools

import jax
import jax.numpy as jnp
from jax import lax
from jax.experimental import pallas as pl
from jax.experimental.pallas import tpu as pltpu
from jax.sharding import PartitionSpec as P

BLOCK = 96
LANES = 128
ROWS = 4
SLOTS_X = 5
COLS = 8
SLOTS_S = 2
WIDE_X = ROWS * BLOCK // LANES
WIDE_S = COLS * BLOCK // LANES
DATA_X = WIDE_X * SLOTS_X * BLOCK
DATA_S = WIDE_S * SLOTS_S * BLOCK
META = 16
WIRE_X = DATA_X + META
WIRE_S = DATA_S + META
SPLIT_X = (0, 720, WIRE_X)
SPLIT_S = (0, 672, WIRE_S)
MESH = pl.DeviceIdType.MESH
AROUND = (0, 1, 3, 2)
HALVES = (0, 1)
OWN = {0: 0, 1: 1, -1: 2, 2: 3, -2: 4, 3: 5, -3: 6, 4: 7}
OTHER = {0: 8, 1: 9, -1: 10, 2: 12, -2: 13, 4: 14}
BY_PAIR, BY_RING = 11, 15


def x_slot(other, dx, sibling=0):
    return 8 * other + 2 * AROUND.index(dx % 4) + sibling


def div(number, by):
    return lax.div(number, jnp.int32(by))


def rem(number, by):
    return lax.rem(number, jnp.int32(by))


def nt(left, right):
    return lax.dot_general(
        left, right, (((1,), (1,)), ((), ())), preferred_element_type=jnp.float32
    )


def kernel(
    a_cols_in, a_count_in, b_cols_in, b_count_in, x_in, s_in, out_ref,
    a_cols, a_count, b_cols, b_count, scalars_came, x_tiles, s_tiles, x_dense, s_dense, total, meta, x_recv, s_recv, sent,
):
    row, col = lax.axis_index("row"), lax.axis_index("col")
    y, z_lo = rem(row, 8), div(row, 8)
    core, z_hi, x = rem(col, 2), rem(div(col, 2), 2), div(col, 4)
    parity = rem(z_lo, 2)

    def at(x_at, y_at, z_lo_at, z_hi_at, core_at):
        return (z_lo_at * 8 + y_at, (x_at * 2 + z_hi_at) * 2 + core_at)

    def along_x(d):
        return at(rem(x + d + 4, 4), y, z_lo, z_hi, core)

    def along_y(d):
        return at(x, rem(y + d + 8, 8), z_lo, z_hi, core)

    pair_chip = at(x, y, z_lo + 1 - 2 * parity, z_hi, core)
    far_chip = at(x, y, z_lo, 1 - z_hi, core)
    sibling = at(x, y, z_lo, z_hi, 1 - core)
    near_chips = (along_x(1), along_x(-1), along_y(1), along_y(-1), pair_chip, sibling)
    barrier = pltpu.get_barrier_semaphore()

    def greet(device):
        pl.semaphore_signal(barrier, inc=1, device_id=device, device_id_type=MESH)

    for device in near_chips:
        greet(device)
    scalars = [
        pltpu.make_async_copy(source, target, scalars_came.at[index])
        for index, (source, target) in enumerate(
            ((a_cols_in, a_cols), (a_count_in, a_count), (b_cols_in, b_cols), (b_count_in, b_count))
        )
    ]
    for copy in scalars:
        copy.start()

    sends = []

    def s_part(slot, half):
        start = SPLIT_S[half]
        return s_tiles.at[slot, pl.ds(start, SPLIT_S[half + 1] - start)]

    def x_part(slot, half):
        start = SPLIT_X[half]
        return x_tiles.at[slot, pl.ds(start, SPLIT_X[half + 1] - start)]

    def send(part, arrived, source, target, device, half, index=None):
        if index is None:
            index = len(sends)
            sends.append(functools.partial(part, source, half))
        pltpu.make_async_remote_copy(
            src_ref=part(source, half), dst_ref=part(target, half),
            send_sem=sent.at[index], recv_sem=arrived.at[target, half],
            device_id=device, device_id_type=MESH,
        ).start()

    def wait(part, arrived, slot, half):
        ref = part(slot, half)
        pltpu.make_async_remote_copy(
            src_ref=ref, dst_ref=ref, send_sem=sent.at[0], recv_sem=arrived.at[slot, half],
            device_id=sibling, device_id_type=MESH,
        ).wait_recv()

    s_copy = functools.partial(send, s_part, s_recv)
    x_copy = functools.partial(send, x_part, x_recv)
    s_wait = functools.partial(wait, s_part, s_recv)
    x_wait = functools.partial(wait, x_part, x_recv)

    lane = lax.broadcasted_iota(jnp.int32, (1, LANES), 1)
    unit = (
        lax.broadcasted_iota(jnp.int32, (BLOCK, BLOCK), 0)
        == lax.broadcasted_iota(jnp.int32, (BLOCK, BLOCK), 1)
    ).astype(jnp.bfloat16)

    def lane_columns(where, number, wide, slot):
        first = wide * LANES // BLOCK
        values = []
        for block in (first, first + 1):
            live = slot < number[block]
            values.append(jnp.where(live, where(block, slot), -1).astype(jnp.float32))
        return jnp.where(lane + wide * LANES < (first + 1) * BLOCK, values[0], values[1])

    for slot in range(SLOTS_S):
        turned = nt(unit, s_in[slot]).astype(jnp.bfloat16)
        for wide in range(WIDE_S):
            index = wide * SLOTS_S + slot
            s_tiles[0, index * BLOCK : (index + 1) * BLOCK, :] = turned[
                :, wide * LANES : (wide + 1) * LANES
            ]
    pl.semaphore_wait(barrier, len(near_chips) + z_hi)
    greet(far_chip)

    def s_start(half):
        s_copy(0, OWN[-1], along_y(1), half)
        s_copy(0, OWN[1], along_y(-1), half)

    s_start(0)
    for copy in scalars:
        copy.wait()
    meta[...] = jnp.full_like(meta, -1.0)
    for wide in range(WIDE_S):
        for slot in range(SLOTS_S):
            index = wide * SLOTS_S + slot
            meta[index : index + 1, :] = lane_columns(
                lambda block, slot: b_cols[slot, block], b_count, wide, slot
            )
    s_tiles[0, DATA_S:, :] = meta[...].astype(jnp.bfloat16)
    s_start(1)

    def s_pair():
        for half in HALVES:
            s_copy(0, OTHER[0], pair_chip, half, N_SENDS - 4 + half)

    pl.when(z_hi == 0)(s_pair)

    for slot in range(SLOTS_X):
        turned = nt(unit, x_in[slot]).astype(jnp.bfloat16)
        for wide in range(WIDE_X):
            index = wide * SLOTS_X + slot
            x_tiles[0, index * BLOCK : (index + 1) * BLOCK, :] = turned[
                :, wide * LANES : (wide + 1) * LANES
            ]

    def x_leave(half):
        x_copy(0, x_slot(1, 0), far_chip, half, N_SENDS - 2 + half)

    def x_leave_late():
        @pl.when(z_hi == 0)
        def _():
            pl.semaphore_wait(barrier, 1)
            for half in HALVES:
                x_leave(half)

    def x_start(half):
        pl.when(z_hi == 1)(functools.partial(x_leave, half))
        x_copy(0, x_slot(0, -1), along_x(1), half)
        x_copy(0, x_slot(0, 1), along_x(-1), half)

    x_start(0)
    meta[...] = jnp.full_like(meta, -1.0)
    for wide in range(WIDE_X):
        for slot in range(SLOTS_X):
            index = wide * SLOTS_X + slot
            meta[index : index + 1, :] = lane_columns(
                lambda block, slot: a_cols[block, slot], a_count, wide, slot
            )
    x_tiles[0, DATA_X:, :] = meta[...].astype(jnp.bfloat16)
    x_start(1)
    for half in HALVES:
        x_copy(0, x_slot(0, 0, 1), sibling, half)
    pl.when(z_hi == 1)(s_pair)
    total[...] = jnp.zeros_like(total)

    def s_ring(slots, near, half):
        for sign in (1, -1):
            here = slots[sign * near]
            s_wait(here, half)
            s_copy(here, slots[sign * (near + 1)], along_y(-sign), half)

    def x_near(other, half):
        for d in (1, -1):
            here = x_slot(other, d)
            x_wait(here, half)
            if (half == 0) == (d == 1):
                x_copy(here, x_slot(other, 2), along_x(-d), half)
            x_copy(here, here + 1, sibling, half)

    def x_across(other):
        here = x_slot(other, 2)
        for half in HALVES:
            x_wait(here, half)
            x_copy(here, here + 1, sibling, half)

    def x_far(half):
        here = x_slot(1, 0)
        x_wait(here, half)
        x_copy(here, x_slot(1, -1), along_x(1), half)
        x_copy(here, x_slot(1, 1), along_x(-1), half)
        x_copy(here, here + 1, sibling, half)

    def x_sibling(other, dx):
        for half in HALVES:
            x_wait(x_slot(other, dx, 1), half)

    pair_third = OWN[-3] - core
    ring_second, other_second = OTHER[2] + core, OTHER[-2] - core
    ring_chip = along_y(2 * core - 1)

    def s_third_first():
        s_wait(OWN[3], 0)
        s_copy(OWN[3], OWN[4], along_y(-1), 0)
        s_wait(OWN[-3], 0)
        s_copy(pair_third, BY_PAIR, pair_chip, 0)

    def s_third_last():
        s_wait(OWN[-3], 1)
        s_copy(OWN[-3], OWN[4], along_y(1), 1)
        s_wait(OWN[3], 1)
        s_copy(pair_third, BY_PAIR, pair_chip, 1)

    def s_other_start():
        for half in HALVES:
            s_wait(OTHER[0], half)
            s_copy(OTHER[0], OTHER[1], along_y(-1), half)
            s_copy(OTHER[0], OTHER[-1], along_y(1), half)

    def s_fourth():
        for half in HALVES:
            s_wait(OWN[4], half)
            s_copy(OWN[4], OTHER[4], pair_chip, half)

    def s_other_second(half):
        s_wait(ring_second, half)
        s_copy(ring_second, BY_RING, ring_chip, half)

    def s_last(slot):
        for half in HALVES:
            s_wait(slot, half)

    left = [0]

    def sends_leave(end):
        for index in range(left[0], end):
            ref = sends[index]()
            pltpu.make_async_remote_copy(
                src_ref=ref, dst_ref=ref, send_sem=sent.at[index], recv_sem=x_recv.at[0, 0],
                device_id=sibling, device_id_type=MESH,
            ).wait_send()
        left[0] = end

    part = functools.partial
    plan = (
        "S", "X",
        part(s_ring, OWN, 1, 0), x_leave_late, part(x_sibling, 0, 0), "X",
        part(s_ring, OWN, 1, 1), "S", "S",
        part(s_ring, OWN, 2, 0), part(x_near, 0, 0), part(x_near, 0, 1), "X",
        part(s_ring, OWN, 2, 1), "S", "S",
        part(x_sibling, 0, 1), "X", "X",
        s_third_first, part(x_sibling, 0, -1), "X", part(x_across, 0), s_third_last, part(x_far, 0), "S", "S",
        s_other_start, "X", part(x_sibling, 0, 2), "X",
        s_fourth, part(x_far, 1), part(sends_leave, 20), "S", "S",
        "X", part(s_ring, OTHER, 1, 0), part(x_near, 1, 0), part(x_sibling, 1, 0), "X",
        part(s_ring, OTHER, 1, 1), part(x_near, 1, 1), "S", "S", "X",
        part(s_other_second, 0), part(x_sibling, 1, 1), "X", "X", part(s_last, BY_PAIR), "S",
        part(x_sibling, 1, -1), "X", part(x_across, 1), "X",
        part(s_other_second, 1), part(sends_leave, 40),
        part(s_last, other_second), "S", "S",
        part(x_sibling, 1, 2), "X",
        part(s_last, OTHER[4]), "S",
        part(s_last, BY_RING), "S",
    )
    events, turns, bits = {}, 0, 0
    for entry in plan:
        if entry in ("S", "X"):
            bits += (entry == "X") << turns
            turns += 1
        else:
            events.setdefault(turns, []).append(entry)
    low_bits, high_bits = bits % 2**16, bits // 2**16
    third = 3 - 6 * core

    def distance(s_at):
        h = rem(s_at, 8)
        own = div(h + 1, 2) * (2 * rem(h, 2) - 1)
        tail = jnp.where(h == 3, -third, jnp.where(h == 7, third, jnp.where(h == 6, 4, 18 - 4 * h)))
        return jnp.where((s_at >= 8) & (h >= 3), tail, own)

    def s_row(s_at):
        return rem(parity + div(s_at, 8), 2) * 8 + rem(y + distance(s_at) + 8, 8)

    def x_for_s(s_at):
        t = rem(s_row(s_at) + col - row + 32, 16)
        dx = rem(div(t, 4) - x + 4, 4)
        place = jnp.where(dx == 3, 2, jnp.where(dx == 2, 3, dx))
        far = rem(div(t, 2) + z_hi, 2)
        return far * 8 + place * 2 + rem(t + core, 2)

    def s_for_x(x_at):
        place = rem(div(x_at, 2), 4)
        dx = jnp.where(place == 3, 2, jnp.where(place == 2, 3, place))
        t = rem(x + dx, 4) * 4 + rem(z_hi + div(x_at, 8), 2) * 2 + rem(core + x_at, 2)
        u = rem(t + row - col + 16, 16)
        dy = rem(u - y + 8, 8)
        dy = jnp.where(dy > 4, dy - 8, dy)
        own = jnp.where(dy > 0, 2 * dy - 1, -2 * dy)
        tail = jnp.where(dy == third, 7, jnp.where(dy == -third, 3, jnp.where(dy == 4, 6, own + 1)))
        tail = jnp.where(own < 3, own, tail)
        return jnp.where(rem(div(u, 8) + parity, 2) == 1, 8 + tail, own)

    def multiply(s_at, x_at):
        names = x_tiles[x_at, DATA_X:, :]
        for wide in range(WIDE_X):
            stored, column = [], []
            for slot in range(SLOTS_X):
                index = wide * SLOTS_X + slot
                stored.append(x_tiles[x_at, index * BLOCK : (index + 1) * BLOCK, :])
                column.append(jnp.broadcast_to(names[index : index + 1, :], (BLOCK, LANES)))
            for j in range(COLS):
                placed = jnp.zeros((BLOCK, LANES), jnp.bfloat16)
                for slot in range(SLOTS_X):
                    placed = jnp.where(column[slot] == j, stored[slot], placed)
                x_dense[j * BLOCK : (j + 1) * BLOCK, wide * LANES : (wide + 1) * LANES] = placed
        names = s_tiles[s_at, DATA_S:, :]
        for wide in range(WIDE_S):
            stored, column = [], []
            for slot in range(SLOTS_S):
                index = wide * SLOTS_S + slot
                stored.append(s_tiles[s_at, index * BLOCK : (index + 1) * BLOCK, :])
                column.append(jnp.broadcast_to(names[index : index + 1, :], (BLOCK, LANES)))
            for j in range(COLS):
                placed = jnp.zeros((BLOCK, LANES), jnp.bfloat16)
                for slot in range(SLOTS_S):
                    placed = jnp.where(column[slot] == j, stored[slot], placed)
                s_dense[j * BLOCK : (j + 1) * BLOCK, wide * LANES : (wide + 1) * LANES] = placed
        total[...] += jnp.dot(s_dense[...], x_dense[...], preferred_element_type=jnp.float32)

        @pl.when(s_row(s_at) == 0)
        def _():
            total[...] -= 3.0 * x_dense[...].astype(jnp.float32)

    def happen(step, first, last):
        if last - first == 1:
            for entry in events.get(first, ()):
                entry()
        elif any(first <= turn < last for turn in events):
            middle = (first + last) // 2
            lax.cond(
                step < middle,
                lambda: happen(step, first, middle),
                lambda: happen(step, middle, last),
            )

    def body(step, arrived):
        s_count, x_count = arrived
        happen(step, 0, turns)
        by_x = (jnp.where(step < 16, low_bits, high_bits) >> rem(step, 16)) & 1
        s_at = jnp.where(by_x == 1, s_for_x(x_count), s_count)
        x_at = jnp.where(by_x == 1, x_count, x_for_s(s_count))
        ready = jnp.where(by_x == 1, s_at < s_count, x_at < x_count)

        @pl.when(ready)
        def _():
            multiply(s_at, x_at)

        return s_count + 1 - by_x, x_count + by_x

    lax.fori_loop(0, turns, body, (jnp.int32(0), jnp.int32(0)))
    out_ref[...] = (-0.5 * total[...]).astype(jnp.bfloat16)
    sends.extend(functools.partial(s_part, 0, half) for half in HALVES)
    sends.extend(functools.partial(x_part, 0, half) for half in HALVES)
    assert len(sends) == N_SENDS, len(sends)
    sends_leave(N_SENDS)


N_SENDS = 60


def shards(a_vals, a_cols, a_count, b_vals, b_cols, b_count):
    x_in = a_vals.reshape(ROWS, SLOTS_X, BLOCK, BLOCK).transpose(1, 0, 2, 3)
    x_in = x_in.reshape(SLOTS_X, ROWS * BLOCK, BLOCK)
    b_vals, x_in = lax.optimization_barrier((b_vals, x_in))
    s_in = b_vals.reshape(COLS, SLOTS_S, BLOCK, BLOCK).transpose(1, 0, 2, 3)
    s_in = s_in.reshape(SLOTS_S, COLS * BLOCK, BLOCK)
    blocks = pl.BlockSpec(memory_space=pltpu.VMEM)
    turned = pl.pallas_call(
        kernel,
        out_shape=jax.ShapeDtypeStruct((COLS * BLOCK, ROWS * BLOCK), jnp.bfloat16),
        in_specs=[pl.BlockSpec(memory_space=pl.ANY)] * 4 + [blocks] * 2,
        out_specs=blocks,
        scratch_shapes=[
            pltpu.SMEM((ROWS, SLOTS_X), jnp.int32),
            pltpu.SMEM((ROWS,), jnp.int32),
            pltpu.SMEM((SLOTS_S, COLS), jnp.int32),
            pltpu.SMEM((COLS,), jnp.int32),
            pltpu.SemaphoreType.DMA((4,)),
            pltpu.VMEM((16, WIRE_X, LANES), jnp.bfloat16),
            pltpu.VMEM((16, WIRE_S, LANES), jnp.bfloat16),
            pltpu.VMEM((COLS * BLOCK, ROWS * BLOCK), jnp.bfloat16),
            pltpu.VMEM((COLS * BLOCK, COLS * BLOCK), jnp.bfloat16),
            pltpu.VMEM((COLS * BLOCK, ROWS * BLOCK), jnp.float32),
            pltpu.VMEM((META, LANES), jnp.float32),
            pltpu.SemaphoreType.DMA((16, 2)),
            pltpu.SemaphoreType.DMA((16, 2)),
            pltpu.SemaphoreType.DMA((N_SENDS,)),
        ],
        compiler_params=pltpu.CompilerParams(
            collective_id=0, has_side_effects=True, vmem_limit_bytes=40 * 1024 * 1024
        ),
        name="gather_multiply",
    )(
        *(
            pltpu.with_memory_space_constraint(number, pltpu.HBM)
            for number in (a_cols[0, 0], a_count[0, 0], b_cols[0, 0].T, b_count[0, 0])
        ),
        x_in,
        s_in,
    )
    return turned.T


def solution(mesh):
    in_specs = (
        P("row", "col", None, None, None),
        P("row", "col", None, None),
        P("row", "col", None),
        P("row", "col", None, None, None),
        P("row", "col", None, None),
        P("row", "col", None),
    )
    out_specs = P("row", "col")
    return jax.shard_map(shards, mesh=mesh, in_specs=in_specs, out_specs=out_specs, check_vma=False)
```
